32 devices in a mesh: lat: 4 (over y, x), lon: 8 (over z, core).
Axes of the slice: x: 2, y: 2, z: 4, core: 2. Of those that a mesh axis runs over, the one named last changes fastest.
Arguments:
- field_in: bfloat16 [128, 512, 256], P('lat', 'lon'), may hold values from -6 to 6
- kernel_one: bfloat16 [3, 3, 256, 256], replicated, may hold values from -0.125 to 0.125
- kernel_two: bfloat16 [3, 3, 256, 256], replicated, may hold values from -0.125 to 0.125
- cotangent: bfloat16 [128, 512, 256], P('lat', 'lon'), may hold values from -6 to 6
Outputs:
- field_out: bfloat16 [128, 512, 256], P('lat', 'lon')
- grad_in: bfloat16 [128, 512, 256], P('lat', 'lon')
- grad_kernel_one: float32 [3, 3, 256, 256], replicated
- grad_kernel_two: float32 [3, 3, 256, 256], replicated
The draws below stay inside these ranges and needn't reach their ends.
All inputs are finite; a program needn't handle non-finite values.
Results may differ from the reference program's by a relative error of at most 0.0056.
Values may be sent and summed in bfloat16 or wider, within the bound.
No kernel may reach another device: no remote copies, remote signals or barrier semaphores. Data moves between devices by JAX's collectives and lax.ppermute only.
A program may use at most 128 MiB of HBM per device.

```python
import jax
import jax.numpy as jnp

C = 256
NLAT = 128
NLON = 512


def level_of(own_key, extent, pieces, low, high):
    loudness = 1.0
    for dim, parts in pieces:
        steps = jax.random.uniform(jax.random.fold_in(jax.random.fold_in(own_key, 6), dim), (parts,), jnp.float32, low / len(pieces), high / len(pieces))
        loudness = loudness * jnp.repeat(jnp.exp(steps), extent[dim] // parts).reshape((-1,) + (1,) * (len(extent) - 1 - dim))
    return loudness


def centred(key, extent, deviation, bound, pieces=(), kind=jnp.bfloat16):
    loudness = level_of(key, extent, pieces, -0.22, 0.18) if pieces else 1.0
    result = jax.random.normal(key, extent, jnp.float32) * deviation * loudness
    return jnp.minimum(jnp.maximum(result, -bound), bound).astype(kind)


def setup_inputs(seed: int = 0) -> dict:
    key_of = jax.random.split(jax.random.key(seed), 5)
    return {
        "field_in": centred(key_of[0], (NLAT, NLON, C), 1.0, 6.0, ((0, 4), (1, 8))),
        "kernel_one": centred(key_of[1], (3, 3, C, C), (9 * C) ** -0.5, 0.125),
        "kernel_two": centred(key_of[2], (3, 3, C, C), (9 * C) ** -0.5, 0.125),
        "cotangent": centred(key_of[3], (NLAT, NLON, C), 1.0, 6.0, ((0, 4), (1, 8))),
    }


def silu_grad(value):
    sig = jax.nn.sigmoid(value)
    return sig * (1.0 + value * (1.0 - sig))

def extend(field):
    wrapped = jnp.pad(field, ((0, 0), (1, 1), (0, 0)), mode='wrap')
    return jnp.pad(wrapped, ((1, 1), (0, 0), (0, 0)))

def conv(padded, kernel, rows, cols):
    chans = padded.shape[2]
    total = jnp.zeros((rows * cols, kernel.shape[3]), jnp.float32)
    for i in range(3):
        for j in range(3):
            piece = padded[i:i + rows, j:j + cols, :].reshape(rows * cols, chans)
            total = total + jnp.dot(piece, kernel[i, j], preferred_element_type=jnp.float32)
    return total.reshape(rows, cols, kernel.shape[3])

def conv_t(padded, kernel, rows, cols):
    chans = padded.shape[2]
    total = jnp.zeros((rows * cols, kernel.shape[2]), jnp.float32)
    for i in range(3):
        for j in range(3):
            piece = padded[2 - i:2 - i + rows, 2 - j:2 - j + cols, :].reshape(rows * cols, chans)
            total = total + jnp.dot(piece, kernel[i, j].T, preferred_element_type=jnp.float32)
    return total.reshape(rows, cols, kernel.shape[2])

def kernel_grad(padded, grad, rows, cols):
    chans = padded.shape[2]
    flat = grad.reshape(rows * cols, grad.shape[2])
    taps = []
    for i in range(3):
        line = []
        for j in range(3):
            piece = padded[i:i + rows, j:j + cols, :].reshape(rows * cols, chans)
            line.append(jax.lax.dot_general(piece, flat, (((0,), (0,)), ((), ())), preferred_element_type=jnp.float32))
        taps.append(jnp.stack(line))
    return jnp.stack(taps)

def reference(field_in, kernel_one, kernel_two, cotangent):
    rows, cols = (field_in.shape[0], field_in.shape[1])
    inner = field_in.astype(jnp.float32)
    act = jax.nn.silu(inner).astype(jnp.bfloat16)
    padded_act = extend(act)
    hid = conv(padded_act, kernel_one, rows, cols)
    mid = jax.nn.silu(hid).astype(jnp.bfloat16)
    padded_mid = extend(mid)
    field_out = (inner + conv(padded_mid, kernel_two, rows, cols)).astype(jnp.bfloat16)
    grad_mid = conv_t(extend(cotangent), kernel_two, rows, cols)
    grad_hid = (grad_mid * silu_grad(hid)).astype(jnp.bfloat16)
    grad_act = conv_t(extend(grad_hid), kernel_one, rows, cols)
    grad_in = (cotangent.astype(jnp.float32) + grad_act * silu_grad(inner)).astype(jnp.bfloat16)
    factor = float(rows * cols) ** (-0.5)
    grad_two = kernel_grad(padded_mid, cotangent, rows, cols) * factor
    grad_one = kernel_grad(padded_act, grad_hid, rows, cols) * factor
    return (field_out, grad_in, grad_one, grad_two)
```

```python
import jax
import jax.numpy as jnp
from jax import lax
from jax.sharding import PartitionSpec as P

BOTH = ("lat", "lon")


def silu_grad(value):
    sig = jax.nn.sigmoid(value)
    return sig * (1.0 + value * (1.0 - sig))


def convolve(padded, kernel, dims):
    return lax.conv_general_dilated(
        padded[None],
        kernel,
        (1, 1),
        "VALID",
        dimension_numbers=dims,
        preferred_element_type=jnp.float32,
    )[0]


def conv(padded, kernel):
    return convolve(padded, kernel, ("NHWC", "HWIO", "NHWC"))


def conv_t(padded, kernel):
    return convolve(padded, kernel[::-1, ::-1], ("NHWC", "HWOI", "NHWC"))


def kernel_grad(padded, grad):
    rows, cols, chans = grad.shape
    flat = grad.reshape(rows * cols, chans)
    taps = []
    for i in range(3):
        for j in range(3):
            piece = padded[i : i + rows, j : j + cols, :].reshape(rows * cols, chans)
            taps.append(
                lax.dot_general(
                    piece, flat, (((0,), (0,)), ((), ())), preferred_element_type=jnp.float32
                )
            )
    return jnp.concatenate(taps)


def paired(count, offset, periodic):
    pairs = []
    for low in range(offset, count, 2):
        high = low + 1
        if high == count:
            if not periodic:
                continue
            high = 0
        pairs += [(low, high), (high, low)]
    return pairs


def extended(block, axis, dim, width, periodic):
    count = lax.axis_size(axis)
    odd = lax.axis_index(axis) % 2 == 1
    first = lax.slice_in_dim(block, 0, width, axis=dim)
    last = lax.slice_in_dim(block, block.shape[dim] - width, None, axis=dim)
    near = lax.ppermute(jnp.where(odd, first, last), axis, paired(count, 0, periodic))
    far = lax.ppermute(jnp.where(odd, last, first), axis, paired(count, 1, periodic))
    low = jnp.where(odd, near, far)
    high = jnp.where(odd, far, near)
    return jnp.concatenate([low, block, high], axis=dim)


def log2(count):
    assert count & (count - 1) == 0
    return count.bit_length() - 1


def swap_plan(lat_count, lon_count):
    lon_bits = log2(lon_count)
    flat_bits = lon_bits + log2(lat_count)
    lat = list(range(lon_bits, flat_bits))
    lon = list(range(1, lon_bits))
    even = [0] + lat + lon
    odd = [0] + lat[::-1] + lon
    pairs = [
        [(d, d ^ (1 << (o if d & 1 else e))) for d in range(1 << flat_bits)]
        for e, o in zip(even, odd)
    ]
    return even, odd, pairs


def summed(value):
    lat_count, lon_count = lax.axis_size("lat"), lax.axis_size("lon")
    even, odd, pairs = swap_plan(lat_count, lon_count)
    me = lax.axis_index("lat") * lon_count + lax.axis_index("lon")
    is_odd = me & 1
    bits = [jnp.where(is_odd == 1, (me >> o) & 1, (me >> e) & 1) for e, o in zip(even, odd)]
    count = len(pairs)
    for step in range(count - 1):
        half = value.shape[0] // 2
        keep = lax.dynamic_slice_in_dim(value, bits[step] * half, half)
        send = lax.dynamic_slice_in_dim(value, (1 - bits[step]) * half, half)
        got = lax.ppermute(send.astype(jnp.bfloat16), BOTH, pairs[step])
        value = keep + got.astype(jnp.float32)
    value = value.astype(jnp.bfloat16)
    got = lax.ppermute(value, BOTH, pairs[-1])
    value = (value.astype(jnp.float32) + got.astype(jnp.float32)).astype(jnp.bfloat16)
    for step in range(count - 2, -1, -1):
        got = lax.ppermute(value, BOTH, pairs[step])
        low = jnp.where(bits[step] == 1, got, value)
        high = jnp.where(bits[step] == 1, value, got)
        value = jnp.concatenate([low, high])
    return value.astype(jnp.float32)


def shards(field_in, kernel_one, kernel_two, cotangent):
    rows, cols, chans = field_in.shape
    lat_count, lon_count = lax.axis_size("lat"), lax.axis_size("lon")
    lat = lax.axis_index("lat")
    both = jnp.stack([field_in, cotangent])
    both = extended(both, "lon", 2, 2, True)
    both = extended(both, "lat", 1, 2, False)
    field, cot = both[0], both[1]
    act = jax.nn.silu(field.astype(jnp.float32)).astype(jnp.bfloat16)
    row = lax.broadcasted_iota(jnp.int32, (rows + 2, 1, 1), 0)
    inside = jnp.logical_and(
        jnp.logical_or(row > 0, lat > 0), jnp.logical_or(row < rows + 1, lat < lat_count - 1)
    )
    hid = conv(act, kernel_one)
    mid = jnp.where(inside, jax.nn.silu(hid), 0.0).astype(jnp.bfloat16)
    shape = (3, 3, chans, chans)
    term_two = kernel_grad(mid, cotangent)
    sum_two = summed(term_two)
    grad_mid = conv_t(cot, kernel_two)
    grad_hid = jnp.where(inside, grad_mid * silu_grad(hid), 0.0).astype(jnp.bfloat16)
    term_one = kernel_grad(act[1:-1, 1:-1], grad_hid[1:-1, 1:-1])
    sum_one = summed(term_one)
    inner = field_in.astype(jnp.float32)
    field_out = (inner + conv(mid, kernel_two)).astype(jnp.bfloat16)
    grad_act = conv_t(grad_hid, kernel_one)
    grad_in = (cotangent.astype(jnp.float32) + grad_act * silu_grad(inner)).astype(jnp.bfloat16)
    factor = float(rows * lat_count * cols * lon_count) ** (-0.5)
    return (
        field_out,
        grad_in,
        (sum_one * factor).reshape(shape),
        (sum_two * factor).reshape(shape),
    )


def solution(mesh):
    return jax.shard_map(
        shards,
        mesh=mesh,
        in_specs=(P("lat", "lon", None), P(), P(), P("lat", "lon", None)),
        out_specs=(P("lat", "lon", None), P("lat", "lon", None), P(), P()),
        check_vma=False,
    )
```

```python
import functools

import jax
import jax.numpy as jnp
from jax import lax
from jax.experimental import pallas as pl
from jax.experimental.pallas import tpu as pltpu
from jax.sharding import PartitionSpec as P

BOTH = ("lat", "lon")
F32, BF16 = jnp.float32, jnp.bfloat16


def kernel_call(body, name, outs, ins, flops=0, scratch=(), aliases=None, limit=24):
    out_shape, out_specs, in_specs, arrays = [], [], [], []
    for shape, kind, *place in outs:
        out_shape.append(pltpu.HBM(shape, kind) if place else pltpu.VMEM(shape, kind))
        out_specs.append(pl.BlockSpec(memory_space=pltpu.HBM if place else pltpu.VMEM))
    for x in ins:
        far = isinstance(x, tuple)
        arrays.append(x[0] if far else x)
        in_specs.append(pl.BlockSpec(memory_space=pltpu.HBM if far else pltpu.VMEM))
    moved = sum(x.size * x.dtype.itemsize for x in arrays)
    return pl.pallas_call(
        body,
        out_shape=out_shape,
        in_specs=in_specs,
        out_specs=out_specs,
        scratch_shapes=list(scratch),
        input_output_aliases=aliases or {},
        compiler_params=pltpu.CompilerParams(vmem_limit_bytes=limit << 20),
        cost_estimate=pl.CostEstimate(flops=flops, bytes_accessed=moved, transcendentals=0),
        name=name,
    )(*arrays)


def in_hbm(x):
    return (pltpu.with_memory_space_constraint(x, pltpu.HBM),)


def sigmoid(value):
    return 1.0 / (1.0 + jnp.exp(-value))


def silu(value):
    return value / (1.0 + jnp.exp(-value))


def same(value):
    return value


def silu_grad(value):
    sig = sigmoid(value)
    return sig * (1.0 + value * (1.0 - sig))


def aligned(start, step):
    return pl.multiple_of(start, step)


def is_odd(axis):
    return lax.axis_index(axis) % 2 == 1


def put_shifted(out, start, x, cols, left=None, right=None):
    chans = x.shape[1]
    col = lax.broadcasted_iota(jnp.int32, x.shape, 0)
    before = pltpu.roll(x, 1, 0)
    after = pltpu.roll(x, cols - 1, 0)
    if left is not None:
        before = jnp.where(col == 0, left, before)
        after = jnp.where(col == cols - 1, right, after)
    where = pl.ds(start, cols)
    out[where, :chans] = before.astype(BF16)
    out[where, chans : 2 * chans] = x.astype(BF16)
    out[where, 2 * chans :] = after.astype(BF16)


def conv_rows(shifted, weights, start, count, cols):
    piece = jnp.concatenate([shifted[pl.ds(start + i * cols, count), :] for i in range(3)], axis=1)
    return jnp.dot(piece, weights[...], preferred_element_type=F32)


def ends_kernel(cols, field_hbm, cot_hbm, field, cot, near, far, lines, sems):
    rows = field.shape[0] // cols
    copies = [
        pltpu.make_async_copy(field_hbm, field, sems.at[0]),
        pltpu.make_async_copy(cot_hbm, cot, sems.at[1]),
    ]
    for copy in copies:
        copy.start()
    odd = is_odd("lon")
    for n, (copy, source) in enumerate(zip(copies, (field, cot))):
        copy.wait()
        for r in range(rows):
            first = source[r * cols : r * cols + 16, :].astype(F32)[:1]
            last = source[(r + 1) * cols - 16 : (r + 1) * cols, :].astype(F32)[15:]
            lines[n * rows + r : n * rows + r + 1, :] = jnp.where(odd, first, last)
            lines[(2 + n) * rows + r : (2 + n) * rows + r + 1, :] = jnp.where(odd, last, first)
    near[...] = lines[: 2 * rows, :].astype(BF16)
    far[...] = lines[2 * rows :, :].astype(BF16)


def prep_kernel(cols, field, one_hbm, two_hbm, act3, k_one, k_two, t_one, t_two, sems):
    rows = field.shape[0] // cols
    chans = field.shape[1]
    copies = [
        pltpu.make_async_copy(one_hbm, k_one, sems.at[0]),
        pltpu.make_async_copy(two_hbm, k_two, sems.at[1]),
    ]
    for copy in copies:
        copy.start()

    def body(r, carry):
        at = aligned(r * cols, cols)
        to = aligned((r + 1) * cols, cols)
        put_shifted(act3, to, silu(field[pl.ds(at, cols), :].astype(F32)), cols)
        return carry

    lax.fori_loop(0, rows, body, 0, unroll=2)
    for copy in copies:
        copy.wait()
    for tap in range(9):
        to = slice((8 - tap) * chans, (9 - tap) * chans)
        at = slice(tap * chans, (tap + 1) * chans)
        t_one[to, :] = k_one[at, :].T
        t_two[to, :] = k_two[at, :].T


def edge_kernel(cols, field, cot, near, far, send_near, send_far):
    rows = field.shape[0] // cols
    chans = field.shape[1]
    odd = is_odd("lon")
    odd_lat = lax.axis_index("lat") % 2
    low, high = near[...].astype(F32), far[...].astype(F32)
    left, right = jnp.where(odd, low, high), jnp.where(odd, high, low)
    for out, first in ((send_near, odd_lat), (send_far, 1 - odd_lat)):
        start = aligned((1 - first) * (rows - 2) * cols, cols)
        out[: 2 * cols, :] = field[pl.ds(start, 2 * cols), :]
        out[2 * cols : 4 * cols, :] = cot[pl.ds(start, 2 * cols), :]
        lines = []
        for base in (0, rows):
            for r in range(2):
                for side in (left, right):
                    top = side[base + r : base + r + 1]
                    bottom = side[base + rows - 2 + r : base + rows - 1 + r]
                    lines.append(jnp.where(first == 1, top, bottom))
        lines.append(jnp.zeros((8, chans), F32))
        out[4 * cols :, :] = jnp.concatenate(lines, axis=0).astype(BF16)


def inner_kernel(cols, near, far, cot, k_one, _a, act3, cot3, hid, mid, turned, edges):
    rows = near.shape[0] // 2
    chans = near.shape[1]
    odd = is_odd("lon")
    low, high = near[...].astype(F32), far[...].astype(F32)
    edges[: 2 * rows, :] = jnp.where(odd, low, high)
    edges[2 * rows :, :] = jnp.where(odd, high, low)
    line = lax.broadcasted_iota(jnp.int32, (16, chans), 0)

    def patch(r, carry):
        start = aligned((r + 1) * cols, cols)
        end = aligned((r + 2) * cols - 16, 16)
        left = silu(edges[pl.ds(r, 1), :]).astype(BF16).astype(F32)
        right = silu(edges[pl.ds(2 * rows + r, 1), :]).astype(BF16).astype(F32)
        old = act3[pl.ds(start, 16), :chans].astype(F32)
        act3[pl.ds(start, 16), :chans] = jnp.where(line == 0, left, old).astype(BF16)
        old = act3[pl.ds(end, 16), 2 * chans :].astype(F32)
        act3[pl.ds(end, 16), 2 * chans :] = jnp.where(line == 15, right, old).astype(BF16)
        x = cot[pl.ds(aligned(r * cols, cols), cols), :].astype(F32)
        left, right = edges[pl.ds(rows + r, 1), :], edges[pl.ds(3 * rows + r, 1), :]
        put_shifted(cot3, start, x, cols, left, right)
        return carry

    lax.fori_loop(0, rows, patch, 0, unroll=4)
    for r, count in row_blocks(1, rows - 1):
        to = pl.ds((r + 1) * cols, count * cols)
        got = conv_rows(act3, k_one, r * cols, count * cols, cols)
        hid[to, :] = got
        mid[to, :] = silu(got).astype(BF16)
    own = slice(3 * cols, (rows - 1) * cols)
    turned[:, 2 * cols : (rows - 2) * cols] = mid[own, :].T


def row_blocks(first, end):
    count = -(-(end - first) // 3)
    return [(r, min(count, end - r)) for r in range(first, end, count)]


def halo_rows(near, far):
    odd = is_odd("lat")
    low, high = near[...].astype(F32), far[...].astype(F32)
    return jnp.where(odd, low, high), jnp.where(odd, high, low)


def put_halo(part, halos, n, cols, fix, source):
    rows = source.shape[0] // cols - 2
    for half, halo in enumerate(halos):
        base = half * 4 * cols
        inside = rows - 1 if half else 1
        own = slice(inside * cols, (inside + 2) * cols)
        part[base + (1 - half) * 2 * cols : base + (2 - half) * 2 * cols, :] = source[own, :]
        for r in range(2):
            x = fix(halo[(2 * n + r) * cols : (2 * n + r + 1) * cols])
            corner = 4 * cols + 4 * n + 2 * r
            left, right = fix(halo[corner : corner + 1]), fix(halo[corner + 1 : corner + 2])
            put_shifted(part, base + (half * 2 + r) * cols, x, cols, left, right)


def edge_mask(half, cols, shape):
    lat = lax.axis_index("lat")
    there = lat < lax.axis_size("lat") - 1 if half else lat > 0
    line = lax.broadcasted_iota(jnp.int32, shape, 0)
    inner = line < cols if half else line >= cols
    return jnp.logical_or(inner, there)


def outer_kernel(
    cols, near, far, k_one, _a, _c, _h, _m, _t,
    act3, cot3, hid, mid, turned, keep, send, part, term,
):
    chans = mid.shape[1]
    rows = mid.shape[0] // cols - 2
    halos = halo_rows(near, far)
    put_halo(part, halos, 1, cols, same, cot3)
    cot3[:cols, :] = part[cols : 2 * cols, :]
    cot3[(rows + 1) * cols :, :] = part[6 * cols : 7 * cols, :]
    put_halo(part, halos, 0, cols, silu, act3)
    act3[:cols, :] = part[cols : 2 * cols, :]
    act3[(rows + 1) * cols :, :] = part[6 * cols : 7 * cols, :]
    for half in range(2):
        to = half * rows * cols
        got = conv_rows(part, k_one, half * 4 * cols, 2 * cols, cols)
        hid[to : to + 2 * cols, :] = got
        value = jnp.where(edge_mask(half, cols, got.shape), silu(got), 0.0)
        mid[to : to + 2 * cols, :] = value.astype(BF16)
    turned[:, : 2 * cols] = mid[cols : 3 * cols, :].T
    turned[:, (rows - 2) * cols :] = mid[(rows - 1) * cols : (rows + 1) * cols, :].T
    for i in range(3):
        got = jnp.dot(
            turned[...], cot3[i * cols : (i + rows) * cols, :], preferred_element_type=F32
        )
        for j in range(3):
            tap = (2 - i) * 3 + 2 - j
            term[tap * chans : (tap + 1) * chans, :] = got[:, j * chans : (j + 1) * chans]
    split(term, keep, send)


def split(term, keep, send):
    half = keep.shape[0]
    bit = lax.axis_index("lon") % 2
    keep[...] = term[pl.ds(aligned(bit * half, 16), half), :]
    send[...] = term[pl.ds(aligned((1 - bit) * half, 16), half), :].astype(BF16)


def back_kernel(cols, near, far, t_two, cot3, hid, mid, ghid, turned, side_near, side_far, part, lines):
    chans = mid.shape[1]
    rows = mid.shape[0] // cols - 2
    for r, count in row_blocks(1, rows - 1):
        to = pl.ds((r + 1) * cols, count * cols)
        got = conv_rows(cot3, t_two, r * cols, count * cols, cols)
        ghid[to, :] = (got * silu_grad(hid[to, :])).astype(BF16)
    put_halo(part, halo_rows(near, far), 1, cols, same, cot3)
    for half in range(2):
        to = slice(half * rows * cols, half * rows * cols + 2 * cols)
        got = conv_rows(part, t_two, half * 4 * cols, 2 * cols, cols)
        value = jnp.where(edge_mask(half, cols, got.shape), got * silu_grad(hid[to, :]), 0.0)
        ghid[to, :] = value.astype(BF16)
    turned[...] = ghid[cols : (rows + 1) * cols, :].T
    lanes = side_near.shape[0] // 2
    odd = is_odd("lon")
    for n, source in enumerate((mid, ghid)):
        for r in range(rows + 2):
            first = source[r * cols : r * cols + 16, :].astype(F32)[:1]
            last = source[(r + 1) * cols - 16 : (r + 1) * cols, :].astype(F32)[15:]
            at = n * lanes + r
            lines[at : at + 1, :] = jnp.where(odd, first, last)
            lines[2 * lanes + at : 2 * lanes + at + 1, :] = jnp.where(odd, last, first)
        for base in (n * lanes, (2 + n) * lanes):
            lines[base + rows + 2 : base + lanes, :] = jnp.zeros((lanes - rows - 2, chans), F32)
    side_near[...] = lines[: 2 * lanes, :].astype(BF16)
    side_far[...] = lines[2 * lanes :, :].astype(BF16)


def grad_one_kernel(cols, turned, act3, keep, send, term):
    chans, cells = turned.shape
    for i in range(3):
        got = jnp.dot(
            turned[...], act3[i * cols : i * cols + cells, :], preferred_element_type=F32
        )
        for j in range(3):
            tap = i * 3 + j
            term[tap * chans : (tap + 1) * chans, :] = got[:, j * chans : (j + 1) * chans].T
    split(term, keep, send)


def last_kernel(backward, first, count, cols, near, far, value, weights, field, cot, *rest):
    out, edges, shifted, result, sems = rest[-5:]
    lanes = near.shape[0] // 2
    odd = is_odd("lon")
    part = slice(lanes, None) if backward else slice(0, lanes)
    low, high = near[part, :].astype(F32), far[part, :].astype(F32)
    edges[:lanes, :] = jnp.where(odd, low, high)
    edges[lanes:, :] = jnp.where(odd, high, low)

    def body(r, carry):
        x = value[pl.ds(aligned((first + r) * cols, cols), cols), :].astype(F32)
        left, right = edges[pl.ds(first + r, 1), :], edges[pl.ds(lanes + first + r, 1), :]
        put_shifted(shifted, aligned(r * cols, cols), x, cols, left, right)
        return carry

    lax.fori_loop(0, count + 2, body, 0, unroll=2)
    step = max(count // 2, 1)
    copies = []
    for n, r in enumerate(range(0, count, step)):
        at = slice((first + r) * cols, (first + r + step) * cols)
        to = slice(r * cols, (r + step) * cols)
        got = conv_rows(shifted, weights, r * cols, step * cols, cols)
        x = field[at, :].astype(F32)
        if backward:
            result[to, :] = (cot[at, :].astype(F32) + got * silu_grad(x)).astype(BF16)
        else:
            result[to, :] = (x + got).astype(BF16)
        copies.append(pltpu.make_async_copy(result.at[to, :], out.at[at, :], sems.at[n]))
        copies[-1].start()
    for copy in copies:
        copy.wait()


def step_bit(step):
    lat_count, lon_count = lax.axis_size("lat"), lax.axis_size("lon")
    even, odd, _ = swap_plan(lat_count, lon_count)
    me = lax.axis_index("lat") * lon_count + lax.axis_index("lon")
    return jnp.where(me % 2 == 1, (me >> odd[step]) & 1, (me >> even[step]) & 1)


def halves(bit, half):
    mine = pl.ds(aligned(bit * half, 16), half)
    other = pl.ds(aligned((1 - bit) * half, 16), half)
    return mine, other


def add_split_kernel(step, keep, got, out, send):
    mine, other = halves(step_bit(step), out.shape[0])
    out[...] = keep[mine, :] + got[mine, :].astype(F32)
    send[...] = (keep[other, :] + got[other, :].astype(F32)).astype(BF16)


def add_round_kernel(keep, got, out):
    out[...] = (keep[...].astype(F32) + got[...].astype(F32)).astype(BF16)


def join_kernel(step, value, got, out):
    mine, other = halves(step_bit(step), value.shape[0])
    out[mine, :] = value[...]
    out[other, :] = got[...]


def final_kernel(factor, own, value, *rest):
    out, scaled, sems = rest[-3:]
    half, chunks = value.shape[0], sems.shape[0]
    bit = step_bit(0)
    base = (bit if own else 1 - bit) * half
    copies = []
    for n in range(chunks):
        at = pl.ds(n * (half // chunks), half // chunks)
        to = pl.ds(aligned(base + n * (half // chunks), 16), half // chunks)
        scaled[at, :] = value[at, :].astype(F32) * factor
        copies.append(pltpu.make_async_copy(scaled.at[at, :], out.at[to, :], sems.at[n]))
        copies[-1].start()
    for copy in copies:
        copy.wait()


def paired(count, offset, periodic):
    pairs = []
    for low in range(offset, count, 2):
        high = low + 1
        if high == count:
            if not periodic:
                continue
            high = 0
        pairs += [(low, high), (high, low)]
    return pairs


def log2(count):
    assert count & (count - 1) == 0
    return count.bit_length() - 1


def swap_plan(lat_count, lon_count):
    lon_bits = log2(lon_count)
    lat = list(range(lon_bits, lon_bits + log2(lat_count)))
    lon = list(range(1, lon_bits))
    even = [0] + lat + lon
    odd = [0] + lat[::-1] + lon[::-1]
    pairs = [
        [(d, d ^ (1 << (o if d & 1 else e))) for d in range(lat_count * lon_count)]
        for e, o in zip(even, odd)
    ]
    return even, odd, pairs


def swapped(value, pairs):
    return lax.ppermute(value, BOTH, pairs)


def after(value, *others):
    return lax.optimization_barrier((value, *others))[0]


class Summed:
    def __init__(self, keep, send, pairs, factor):
        self.keep, self.send, self.pairs, self.factor = keep, send, pairs, factor
        self.count, self.step, self.value = len(pairs), 0, None
        self.bits = [step_bit(step) for step in range(self.count)]

    @property
    def sent(self):
        return self.send if self.step < self.count - 1 else self.value

    def start(self):
        step, last = self.step, self.count - 1
        if self.running:
            self.got = swapped(self.sent, self.pairs[step if step <= last else 2 * last - step])

    def finish(self, *others):
        got = after(self.got, *others) if others else self.got
        keep, count, step = self.keep, self.count, self.step
        chans = keep.shape[1]
        self.step += 1
        if step < count - 2:
            half = keep.shape[0] // 2
            if half % 16:
                value = keep + got.astype(F32)
                bit = self.bits[step + 1]
                self.keep = lax.dynamic_slice_in_dim(value, bit * half, half)
                send = lax.dynamic_slice_in_dim(value, (1 - bit) * half, half)
                self.send = send.astype(BF16)
            else:
                body = functools.partial(add_split_kernel, step + 1)
                outs = [((half, chans), F32), ((half, chans), BF16)]
                self.keep, self.send = kernel_call(body, "sum_step", outs, [keep, got], limit=16)
        elif step < count:
            mine = keep if step == count - 2 else self.value
            outs = [(keep.shape, BF16)]
            (self.value,) = kernel_call(add_round_kernel, "sum_round", outs, [mine, got], limit=16)
        else:
            back = 2 * count - 2 - step
            value = self.value
            half = value.shape[0]
            if back == 0:
                out = ((2 * half, chans), F32, "hbm")
                scratch = [pltpu.VMEM((half, chans), F32), pltpu.SemaphoreType.DMA((4,))]
                result = None
                for own in (True, False):
                    body = functools.partial(final_kernel, self.factor, own)
                    x, extra = (value, []) if own else (after(got, result), [0])
                    (result,) = kernel_call(
                        body,
                        "scaled",
                        [out],
                        [x] + [in_hbm(result) for _ in extra],
                        scratch=scratch,
                        aliases={1: 0} if extra else None,
                        limit=16,
                    )
                self.value = result
            elif half % 16:
                low = jnp.where(self.bits[back] == 1, got, value)
                high = jnp.where(self.bits[back] == 1, value, got)
                self.value = jnp.concatenate([low, high])
            else:
                body = functools.partial(join_kernel, back)
                outs = [((2 * half, chans), BF16)]
                (self.value,) = kernel_call(body, "join", outs, [value, got], limit=16)

    @property
    def running(self):
        return self.step < 2 * self.count - 1


def shards(field_in, kernel_one, kernel_two, cotangent):
    rows, cols, chans = field_in.shape
    cells, tall = rows * cols, (rows + 2) * cols
    lat_count, lon_count = lax.axis_size("lat"), lax.axis_size("lon")
    _, _, pairs = swap_plan(lat_count, lon_count)
    factor = float(rows * lat_count * cols * lon_count) ** (-0.5)
    flops = 2 * cells * 9 * chans * chans
    sems = pltpu.SemaphoreType.DMA((2,))

    def call(body, *args, **kwargs):
        return kernel_call(functools.partial(body, cols), *args, **kwargs)

    near_lon, far_lon = paired(lon_count, 0, True), paired(lon_count, 1, True)
    near_lat, far_lat = paired(lat_count, 0, False), paired(lat_count, 1, False)

    tile = ((cells, chans), BF16)
    line = ((2 * rows, chans), BF16)
    field, cot, near, far = call(
        ends_kernel,
        "ends",
        [tile, tile, line, line],
        [in_hbm(field_in.reshape(cells, chans)), in_hbm(cotangent.reshape(cells, chans))],
        scratch=[pltpu.VMEM((4 * rows, chans), F32), sems],
    )
    lon_near = lax.ppermute(near, "lon", near_lon)
    lon_far = lax.ppermute(far, "lon", far_lon)
    wide = ((tall, 3 * chans), BF16)
    square = ((9 * chans, chans), BF16)
    act3, k_one, k_two, t_one, t_two = call(
        prep_kernel,
        "prep",
        [wide, square, square, square, square],
        [field] + [in_hbm(k.reshape(9 * chans, chans)) for k in (kernel_one, kernel_two)],
        flops=flops,
        scratch=[sems],
    )

    strip = ((4 * cols + 16, chans), BF16)
    send_near, send_far = call(
        edge_kernel, "edges", [strip, strip], [field, cot, after(lon_near, act3), lon_far]
    )
    lat_near = lax.ppermute(send_near, "lat", near_lat)
    lat_far = lax.ppermute(send_far, "lat", far_lat)

    high = ((tall, chans), F32)
    flat = ((tall, chans), BF16)
    turned = ((chans, cells), BF16)
    act3, cot3, hid, mid, mid_t = call(
        inner_kernel,
        "inner_rows",
        [wide, wide, high, flat, turned],
        [lon_near, lon_far, cot, k_one, after(act3, send_near, send_far)],
        flops=flops,
        scratch=[pltpu.VMEM((4 * rows, chans), F32)],
        aliases={4: 0},
    )
    half = 9 * chans // 2
    parts = [((half, chans), F32), ((half, chans), BF16)]
    part = pltpu.VMEM((8 * cols, 3 * chans), BF16)
    term = pltpu.VMEM((9 * chans, chans), F32)
    act3, cot3, hid, mid, _, keep, send = call(
        outer_kernel,
        "grad_two",
        [wide, wide, high, flat, turned] + parts,
        [lat_near, lat_far, k_one, act3, cot3, hid, mid, mid_t],
        flops=flops,
        scratch=[part, term],
        aliases={3: 0, 4: 1, 5: 2, 6: 3, 7: 4},
    )
    two = Summed(keep, send, pairs, factor)
    two.start()

    lanes = -(-(rows + 2) // 16) * 16
    sides = ((2 * lanes, chans), BF16)
    ghid, ghid_t, side_near, side_far = call(
        back_kernel,
        "grad_hid",
        [flat, turned, sides, sides],
        [lat_near, lat_far, t_two, cot3, hid, mid],
        flops=flops,
        scratch=[part, pltpu.VMEM((4 * lanes, chans), F32)],
    )
    two.finish(ghid)

    side_near, side_far = after(side_near, two.sent), after(side_far, two.sent)
    two.start()
    side_near = lax.ppermute(side_near, "lon", near_lon)
    side_far = lax.ppermute(side_far, "lon", far_lon)
    keep, send = call(
        grad_one_kernel,
        "grad_one",
        parts,
        [after(ghid_t, two.sent), act3],
        flops=flops,
        scratch=[term],
    )
    side_near, side_far = after(side_near, keep), after(side_far, keep)
    two.finish(keep)
    one = Summed(keep, after(send, two.sent, side_near, side_far), pairs, factor)
    one.start()
    two.start()

    results = [None, None]
    pieces = [(0, 0), (0, 1), (1, 0), (1, 1)]

    def piece(which, part, *others):
        count = rows // 2
        old = results[which]
        ins = [side_near, side_far, after((mid, ghid)[which], *others)]
        ins += [(k_two, t_one)[which], field, cot]
        (results[which],) = call(
            functools.partial(last_kernel, bool(which), part * count, count),
            ("field_out", "grad_in")[which],
            [((cells, chans), BF16, "hbm")],
            ins + ([in_hbm(old)] if part else []),
            flops=flops // 2,
            scratch=[
                pltpu.VMEM((2 * lanes, chans), F32),
                pltpu.VMEM(((count + 2) * cols, 3 * chans), BF16),
                pltpu.VMEM((count * cols, chans), BF16),
                sems,
            ],
            aliases={len(ins): 0} if part else None,
        )
        return results[which]

    for which, half in pieces:
        fill = piece(which, half, one.sent, two.sent)
        one.finish(fill)
        two.finish(fill, one.sent)
        one.start()
        two.start()
    while one.running:
        one.finish(two.sent)
        one.start()
        if two.running:
            two.finish(one.sent)
            two.start()
    shape = (3, 3, chans, chans)
    return (
        results[0].reshape(rows, cols, chans),
        results[1].reshape(rows, cols, chans),
        one.value.reshape(shape),
        two.value.reshape(shape),
    )


def solution(mesh):
    return jax.shard_map(
        shards,
        mesh=mesh,
        in_specs=(P("lat", "lon", None), P(), P(), P("lat", "lon", None)),
        out_specs=(P("lat", "lon", None), P("lat", "lon", None), P(), P()),
        check_vma=False,
    )
```

```python
import functools

import jax
import jax.numpy as jnp
from jax import lax
from jax.experimental import pallas as pl
from jax.experimental.pallas import tpu as pltpu
from jax.sharding import PartitionSpec as P

BOTH = ("lat", "lon")
F32, BF16 = jnp.float32, jnp.bfloat16


def kernel_call(body, name, outs, ins, flops=0, scratch=(), aliases=None, limit=24):
    out_shape, out_specs, in_specs, arrays = [], [], [], []
    for shape, kind, *place in outs:
        out_shape.append(pltpu.HBM(shape, kind) if place else pltpu.VMEM(shape, kind))
        out_specs.append(pl.BlockSpec(memory_space=pltpu.HBM if place else pltpu.VMEM))
    for x in ins:
        far = isinstance(x, tuple)
        arrays.append(x[0] if far else x)
        in_specs.append(pl.BlockSpec(memory_space=pltpu.HBM if far else pltpu.VMEM))
    moved = sum(x.size * x.dtype.itemsize for x in arrays)
    return pl.pallas_call(
        body,
        out_shape=out_shape,
        in_specs=in_specs,
        out_specs=out_specs,
        scratch_shapes=list(scratch),
        input_output_aliases=aliases or {},
        compiler_params=pltpu.CompilerParams(vmem_limit_bytes=limit << 20),
        cost_estimate=pl.CostEstimate(flops=flops, bytes_accessed=moved, transcendentals=0),
        name=name,
    )(*arrays)


def in_hbm(x):
    return (pltpu.with_memory_space_constraint(x, pltpu.HBM),)


def sigmoid(value):
    return 1.0 / (1.0 + jnp.exp(-value))


def silu(value):
    return value / (1.0 + jnp.exp(-value))


def same(value):
    return value


def silu_grad(value):
    sig = sigmoid(value)
    return sig * (1.0 + value * (1.0 - sig))


def aligned(start, step):
    return pl.multiple_of(start, step)


def is_odd(axis):
    return lax.axis_index(axis) % 2 == 1


def put_shifted(out, start, x, cols, left=None, right=None):
    chans = x.shape[1]
    col = lax.broadcasted_iota(jnp.int32, x.shape, 0)
    before = pltpu.roll(x, 1, 0)
    after = pltpu.roll(x, cols - 1, 0)
    if left is not None:
        before = jnp.where(col == 0, left, before)
        after = jnp.where(col == cols - 1, right, after)
    where = pl.ds(start, cols)
    out[where, :chans] = before.astype(BF16)
    out[where, chans : 2 * chans] = x.astype(BF16)
    out[where, 2 * chans :] = after.astype(BF16)


def conv_rows(shifted, weights, start, count, cols):
    piece = jnp.concatenate([shifted[pl.ds(start + i * cols, count), :] for i in range(3)], axis=1)
    return jnp.dot(piece, weights[...], preferred_element_type=F32)


def ends_kernel(cols, field_hbm, cot_hbm, field, cot, near, far, lines, sems):
    rows = field.shape[0] // cols
    copies = [
        pltpu.make_async_copy(field_hbm, field, sems.at[0]),
        pltpu.make_async_copy(cot_hbm, cot, sems.at[1]),
    ]
    for copy in copies:
        copy.start()
    odd = is_odd("lon")
    for n, (copy, source) in enumerate(zip(copies, (field, cot))):
        copy.wait()
        for r in range(rows):
            first = source[r * cols : r * cols + 16, :].astype(F32)[:1]
            last = source[(r + 1) * cols - 16 : (r + 1) * cols, :].astype(F32)[15:]
            lines[n * rows + r : n * rows + r + 1, :] = jnp.where(odd, first, last)
            lines[(2 + n) * rows + r : (2 + n) * rows + r + 1, :] = jnp.where(odd, last, first)
    near[...] = lines[: 2 * rows, :].astype(BF16)
    far[...] = lines[2 * rows :, :].astype(BF16)


def prep_kernel(cols, field, one_hbm, two_hbm, act3, k_one, k_two, t_one, t_two, sems):
    rows = field.shape[0] // cols
    chans = field.shape[1]
    copies = [
        pltpu.make_async_copy(one_hbm, k_one, sems.at[0]),
        pltpu.make_async_copy(two_hbm, k_two, sems.at[1]),
    ]
    for copy in copies:
        copy.start()

    def body(r, carry):
        at = aligned(r * cols, cols)
        to = aligned((r + 1) * cols, cols)
        put_shifted(act3, to, silu(field[pl.ds(at, cols), :].astype(F32)), cols)
        return carry

    lax.fori_loop(0, rows, body, 0, unroll=2)
    for copy in copies:
        copy.wait()
    for tap in range(9):
        to = slice((8 - tap) * chans, (9 - tap) * chans)
        at = slice(tap * chans, (tap + 1) * chans)
        t_one[to, :] = k_one[at, :].T
        t_two[to, :] = k_two[at, :].T


def edge_kernel(cols, field, cot, near, far, send_near, send_far):
    rows = field.shape[0] // cols
    chans = field.shape[1]
    odd = is_odd("lon")
    odd_lat = lax.axis_index("lat") % 2
    low, high = near[...].astype(F32), far[...].astype(F32)
    left, right = jnp.where(odd, low, high), jnp.where(odd, high, low)
    for out, first in ((send_near, odd_lat), (send_far, 1 - odd_lat)):
        start = aligned((1 - first) * (rows - 2) * cols, cols)
        out[: 2 * cols, :] = field[pl.ds(start, 2 * cols), :]
        out[2 * cols : 4 * cols, :] = cot[pl.ds(start, 2 * cols), :]
        lines = []
        for base in (0, rows):
            for r in range(2):
                for side in (left, right):
                    top = side[base + r : base + r + 1]
                    bottom = side[base + rows - 2 + r : base + rows - 1 + r]
                    lines.append(jnp.where(first == 1, top, bottom))
        lines.append(jnp.zeros((8, chans), F32))
        out[4 * cols :, :] = jnp.concatenate(lines, axis=0).astype(BF16)


def inner_kernel(cols, near, far, cot, k_one, _a, act3, cot3, hid, mid, turned, edges):
    rows = near.shape[0] // 2
    chans = near.shape[1]
    odd = is_odd("lon")
    low, high = near[...].astype(F32), far[...].astype(F32)
    edges[: 2 * rows, :] = jnp.where(odd, low, high)
    edges[2 * rows :, :] = jnp.where(odd, high, low)
    line = lax.broadcasted_iota(jnp.int32, (16, chans), 0)

    def patch(r, carry):
        start = aligned((r + 1) * cols, cols)
        end = aligned((r + 2) * cols - 16, 16)
        left = silu(edges[pl.ds(r, 1), :]).astype(BF16).astype(F32)
        right = silu(edges[pl.ds(2 * rows + r, 1), :]).astype(BF16).astype(F32)
        old = act3[pl.ds(start, 16), :chans].astype(F32)
        act3[pl.ds(start, 16), :chans] = jnp.where(line == 0, left, old).astype(BF16)
        old = act3[pl.ds(end, 16), 2 * chans :].astype(F32)
        act3[pl.ds(end, 16), 2 * chans :] = jnp.where(line == 15, right, old).astype(BF16)
        x = cot[pl.ds(aligned(r * cols, cols), cols), :].astype(F32)
        left, right = edges[pl.ds(rows + r, 1), :], edges[pl.ds(3 * rows + r, 1), :]
        put_shifted(cot3, start, x, cols, left, right)
        return carry

    lax.fori_loop(0, rows, patch, 0, unroll=4)
    for r, count in row_blocks(1, rows - 1):
        to = pl.ds((r + 1) * cols, count * cols)
        got = conv_rows(act3, k_one, r * cols, count * cols, cols)
        hid[to, :] = got
        mid[to, :] = silu(got).astype(BF16)
    own = slice(3 * cols, (rows - 1) * cols)
    turned[:, 2 * cols : (rows - 2) * cols] = mid[own, :].T


def row_blocks(first, end):
    count = -(-(end - first) // 3)
    return [(r, min(count, end - r)) for r in range(first, end, count)]


def halo_rows(near, far):
    odd = is_odd("lat")
    low, high = near[...].astype(F32), far[...].astype(F32)
    return jnp.where(odd, low, high), jnp.where(odd, high, low)


def put_halo(part, halos, n, cols, fix, source):
    rows = source.shape[0] // cols - 2
    for half, halo in enumerate(halos):
        base = half * 4 * cols
        inside = rows - 1 if half else 1
        own = slice(inside * cols, (inside + 2) * cols)
        part[base + (1 - half) * 2 * cols : base + (2 - half) * 2 * cols, :] = source[own, :]
        for r in range(2):
            x = fix(halo[(2 * n + r) * cols : (2 * n + r + 1) * cols])
            corner = 4 * cols + 4 * n + 2 * r
            left, right = fix(halo[corner : corner + 1]), fix(halo[corner + 1 : corner + 2])
            put_shifted(part, base + (half * 2 + r) * cols, x, cols, left, right)


def edge_mask(half, cols, shape):
    lat = lax.axis_index("lat")
    there = lat < lax.axis_size("lat") - 1 if half else lat > 0
    line = lax.broadcasted_iota(jnp.int32, shape, 0)
    inner = line < cols if half else line >= cols
    return jnp.logical_or(inner, there)


def outer_kernel(
    cols, near, far, k_one, _a, _c, _h, _m, _t,
    act3, cot3, hid, mid, turned, keep, send, part, term,
):
    chans = mid.shape[1]
    rows = mid.shape[0] // cols - 2
    halos = halo_rows(near, far)
    put_halo(part, halos, 1, cols, same, cot3)
    cot3[:cols, :] = part[cols : 2 * cols, :]
    cot3[(rows + 1) * cols :, :] = part[6 * cols : 7 * cols, :]
    put_halo(part, halos, 0, cols, silu, act3)
    act3[:cols, :] = part[cols : 2 * cols, :]
    act3[(rows + 1) * cols :, :] = part[6 * cols : 7 * cols, :]
    for half in range(2):
        to = half * rows * cols
        got = conv_rows(part, k_one, half * 4 * cols, 2 * cols, cols)
        hid[to : to + 2 * cols, :] = got
        value = jnp.where(edge_mask(half, cols, got.shape), silu(got), 0.0)
        mid[to : to + 2 * cols, :] = value.astype(BF16)
    turned[:, : 2 * cols] = mid[cols : 3 * cols, :].T
    turned[:, (rows - 2) * cols :] = mid[(rows - 1) * cols : (rows + 1) * cols, :].T
    for i in range(3):
        got = jnp.dot(
            turned[...], cot3[i * cols : (i + rows) * cols, :], preferred_element_type=F32
        )
        for j in range(3):
            tap = (2 - i) * 3 + 2 - j
            term[tap * chans : (tap + 1) * chans, :] = got[:, j * chans : (j + 1) * chans]
    split(term, keep, send)


def split(term, keep, send):
    half = keep.shape[0]
    bit = lax.axis_index("lon") % 2
    keep[...] = term[pl.ds(aligned(bit * half, 16), half), :]
    send[...] = term[pl.ds(aligned((1 - bit) * half, 16), half), :].astype(BF16)


def back_kernel(cols, near, far, t_two, cot3, hid, mid, ghid, turned, side_near, side_far, part, lines):
    chans = mid.shape[1]
    rows = mid.shape[0] // cols - 2
    for r, count in row_blocks(1, rows - 1):
        to = pl.ds((r + 1) * cols, count * cols)
        got = conv_rows(cot3, t_two, r * cols, count * cols, cols)
        ghid[to, :] = (got * silu_grad(hid[to, :])).astype(BF16)
    put_halo(part, halo_rows(near, far), 1, cols, same, cot3)
    for half in range(2):
        to = slice(half * rows * cols, half * rows * cols + 2 * cols)
        got = conv_rows(part, t_two, half * 4 * cols, 2 * cols, cols)
        value = jnp.where(edge_mask(half, cols, got.shape), got * silu_grad(hid[to, :]), 0.0)
        ghid[to, :] = value.astype(BF16)
    turned[...] = ghid[cols : (rows + 1) * cols, :].T
    lanes = side_near.shape[0] // 2
    odd = is_odd("lon")
    for n, source in enumerate((mid, ghid)):
        for r in range(rows + 2):
            first = source[r * cols : r * cols + 16, :].astype(F32)[:1]
            last = source[(r + 1) * cols - 16 : (r + 1) * cols, :].astype(F32)[15:]
            at = n * lanes + r
            lines[at : at + 1, :] = jnp.where(odd, first, last)
            lines[2 * lanes + at : 2 * lanes + at + 1, :] = jnp.where(odd, last, first)
        for base in (n * lanes, (2 + n) * lanes):
            lines[base + rows + 2 : base + lanes, :] = jnp.zeros((lanes - rows - 2, chans), F32)
    side_near[...] = lines[: 2 * lanes, :].astype(BF16)
    side_far[...] = lines[2 * lanes :, :].astype(BF16)


def grad_one_kernel(cols, turned, act3, keep, send, term):
    chans, cells = turned.shape
    for i in range(3):
        got = jnp.dot(
            turned[...], act3[i * cols : i * cols + cells, :], preferred_element_type=F32
        )
        for j in range(3):
            tap = i * 3 + j
            term[tap * chans : (tap + 1) * chans, :] = got[:, j * chans : (j + 1) * chans].T
    split(term, keep, send)


def last_kernel(backward, first, count, cols, near, far, value, weights, field, cot, *rest):
    out, edges, shifted, result, sems = rest[-5:]
    lanes = near.shape[0] // 2
    odd = is_odd("lon")
    part = slice(lanes, None) if backward else slice(0, lanes)
    low, high = near[part, :].astype(F32), far[part, :].astype(F32)
    edges[:lanes, :] = jnp.where(odd, low, high)
    edges[lanes:, :] = jnp.where(odd, high, low)

    def body(r, carry):
        x = value[pl.ds(aligned((first + r) * cols, cols), cols), :].astype(F32)
        left, right = edges[pl.ds(first + r, 1), :], edges[pl.ds(lanes + first + r, 1), :]
        put_shifted(shifted, aligned(r * cols, cols), x, cols, left, right)
        return carry

    lax.fori_loop(0, count + 2, body, 0, unroll=2)
    step = max(count // 2, 1)
    copies = []
    for n, r in enumerate(range(0, count, step)):
        at = slice((first + r) * cols, (first + r + step) * cols)
        to = slice(r * cols, (r + step) * cols)
        got = conv_rows(shifted, weights, r * cols, step * cols, cols)
        x = field[at, :].astype(F32)
        if backward:
            result[to, :] = (cot[at, :].astype(F32) + got * silu_grad(x)).astype(BF16)
        else:
            result[to, :] = (x + got).astype(BF16)
        copies.append(pltpu.make_async_copy(result.at[to, :], out.at[at, :], sems.at[n]))
        copies[-1].start()
    for copy in copies:
        copy.wait()


def place():
    return lax.axis_index("lat"), lax.axis_index("lon") % 2


def partner(n):
    lat, odd = place()
    even_mask, odd_mask = group_masks(lax.axis_size("lat"))[n]
    return lat ^ jnp.where(odd == 1, odd_mask, even_mask)


def chunk(index, rows):
    return pl.ds(aligned(index * rows, 16), rows)


def spread_kernel(keep, got, own, *sends):
    rows = own.shape[0]
    at = chunk(place()[0], rows)
    own[...] = keep[at, :] + got[at, :].astype(F32)
    for n, send in enumerate(sends):
        at = chunk(partner(n), rows)
        send[...] = (keep[at, :] + got[at, :].astype(F32)).astype(BF16)


def add_round_kernel(own, *rest):
    out = rest[-1]
    total = own[...].astype(F32)
    for got in rest[:-1]:
        total = total + got[...].astype(F32)
    out[...] = total.astype(BF16)


def join_kernel(value, *rest):
    out = rest[-1]
    rows = value.shape[0]
    out[chunk(place()[0], rows), :] = value[...]
    for n, got in enumerate(rest[:-1]):
        out[chunk(partner(n), rows), :] = got[...]


def final_kernel(factor, own, value, *rest):
    out, scaled, sems = rest[-3:]
    half, chunks = value.shape[0], sems.shape[0]
    bit = place()[1]
    base = (bit if own else 1 - bit) * half
    copies = []
    for n in range(chunks):
        at = pl.ds(n * (half // chunks), half // chunks)
        to = pl.ds(aligned(base + n * (half // chunks), 16), half // chunks)
        scaled[at, :] = value[at, :].astype(F32) * factor
        copies.append(pltpu.make_async_copy(scaled.at[at, :], out.at[to, :], sems.at[n]))
        copies[-1].start()
    for copy in copies:
        copy.wait()


def paired(count, offset, periodic):
    pairs = []
    for low in range(offset, count, 2):
        high = low + 1
        if high == count:
            if not periodic:
                continue
            high = 0
        pairs += [(low, high), (high, low)]
    return pairs


def log2(count):
    assert count & (count - 1) == 0
    return count.bit_length() - 1


def reversed_bits(value, width):
    return int(format(value, f"0{width}b")[::-1], 2)


def group_masks(count):
    return [(k, reversed_bits(k, log2(count))) for k in range(1, count)]


def flat_pairs(lat_count, lon_count, move):
    pairs = []
    for lat in range(lat_count):
        for lon in range(lon_count):
            to_lat, to_lon = move(lat, lon)
            pairs.append((lat * lon_count + lon, to_lat * lon_count + to_lon))
    return pairs


def after(values, *others):
    return list(lax.optimization_barrier((*values, *others)))[: len(values)]


class Summed:
    def __init__(self, keep, send, factor):
        lat_count, lon_count = lax.axis_size("lat"), lax.axis_size("lon")
        self.keep, self.sent, self.factor, self.result = keep, [send], factor, None
        core = flat_pairs(lat_count, lon_count, lambda lat, lon: (lat, lon ^ 1))
        group = [
            flat_pairs(
                lat_count, lon_count, lambda lat, lon, m=m: (lat ^ (m[1] if lon & 1 else m[0]), lon)
            )
            for m in group_masks(lat_count)
        ]
        width = log2(lon_count) - 1
        line = [
            flat_pairs(
                lat_count,
                lon_count,
                lambda lat, lon, n=n: (lat, lon ^ (2 << (width - 1 - n if lon & 1 else n))),
            )
            for n in range(width)
        ]
        self.steps = [("core", [core]), ("lat", group)]
        self.steps += [("lon", [pairs]) for pairs in line]
        self.steps += [("join", group), ("last", [core])]

    def start(self):
        kind, pairs = self.steps[0]
        sent = self.sent if kind == "lat" else self.sent * len(pairs)
        self.got = [lax.ppermute(x, BOTH, p) for x, p in zip(sent, pairs)]

    def finish(self):
        kind = self.steps.pop(0)[0]
        got, (rows, chans) = self.got, self.keep.shape
        if kind == "core":
            count = lax.axis_size("lat")
            piece = rows // count
            assert piece % 16 == 0
            outs = [((piece, chans), F32)] + [((piece, chans), BF16)] * (count - 1)
            self.keep, *self.sent = kernel_call(
                spread_kernel, "spread", outs, [self.keep, *got], limit=16
            )
        elif kind == "join":
            outs = [((rows * lax.axis_size("lat"), chans), BF16)]
            self.sent = kernel_call(join_kernel, "join", outs, [*self.sent, *got], limit=16)
        elif kind == "last":
            if self.result is None:
                self.scale(self.sent[0], True)
            self.sent = [self.scale(got[0], False)]
        else:
            mine = self.keep if kind == "lat" else self.sent[0]
            outs = [((rows, chans), BF16)]
            self.sent = kernel_call(add_round_kernel, "add", outs, [mine, *got], limit=16)

    def scale(self, value, own):
        rows, chans = value.shape
        ins = [value] if own else [value, in_hbm(self.result)]
        (self.result,) = kernel_call(
            functools.partial(final_kernel, self.factor, own),
            "scaled",
            [((2 * rows, chans), F32, "hbm")],
            ins,
            scratch=[pltpu.VMEM((rows, chans), F32), pltpu.SemaphoreType.DMA((4,))],
            aliases=None if own else {1: 0},
            limit=16,
        )
        return self.result


class Turns:
    def __init__(self):
        self.last = []

    def run(self, work):
        result = work(self.last)
        self.last = list(result)
        return result

    def start(self, chain):
        chain.sent = after(chain.sent, *self.last)
        self.last = list(chain.sent)
        chain.start()

    def finish(self, chain):
        chain.got = after(chain.got, *self.last)
        chain.finish()
        self.last = list(chain.sent)


def shards(field_in, kernel_one, kernel_two, cotangent):
    rows, cols, chans = field_in.shape
    cells, tall = rows * cols, (rows + 2) * cols
    lat_count, lon_count = lax.axis_size("lat"), lax.axis_size("lon")
    factor = float(rows * lat_count * cols * lon_count) ** (-0.5)
    flops = 2 * cells * 9 * chans * chans
    sems = pltpu.SemaphoreType.DMA((2,))

    def call(body, *args, **kwargs):
        return kernel_call(functools.partial(body, cols), *args, **kwargs)

    near_lon, far_lon = paired(lon_count, 0, True), paired(lon_count, 1, True)
    near_lat, far_lat = paired(lat_count, 0, False), paired(lat_count, 1, False)

    tile = ((cells, chans), BF16)
    line = ((2 * rows, chans), BF16)
    field, cot, near, far = call(
        ends_kernel,
        "ends",
        [tile, tile, line, line],
        [in_hbm(field_in.reshape(cells, chans)), in_hbm(cotangent.reshape(cells, chans))],
        scratch=[pltpu.VMEM((4 * rows, chans), F32), sems],
    )
    lon_near = lax.ppermute(near, "lon", near_lon)
    lon_far = lax.ppermute(far, "lon", far_lon)
    wide = ((tall, 3 * chans), BF16)
    square = ((9 * chans, chans), BF16)
    act3, k_one, k_two, t_one, t_two = call(
        prep_kernel,
        "prep",
        [wide, square, square, square, square],
        [field] + [in_hbm(k.reshape(9 * chans, chans)) for k in (kernel_one, kernel_two)],
        flops=flops,
        scratch=[sems],
    )

    strip = ((4 * cols + 16, chans), BF16)
    send_near, send_far = call(
        edge_kernel, "edges", [strip, strip], [field, cot, *after([lon_near, lon_far], act3)]
    )
    lat_near = lax.ppermute(send_near, "lat", near_lat)
    lat_far = lax.ppermute(send_far, "lat", far_lat)

    high = ((tall, chans), F32)
    flat = ((tall, chans), BF16)
    turned = ((chans, cells), BF16)
    act3, cot3, hid, mid, mid_t = call(
        inner_kernel,
        "inner_rows",
        [wide, wide, high, flat, turned],
        [lon_near, lon_far, cot, k_one, *after([act3], send_near, send_far)],
        flops=flops,
        scratch=[pltpu.VMEM((4 * rows, chans), F32)],
        aliases={4: 0},
    )
    half = 9 * chans // 2
    parts = [((half, chans), F32), ((half, chans), BF16)]
    part = pltpu.VMEM((8 * cols, 3 * chans), BF16)
    term = pltpu.VMEM((9 * chans, chans), F32)
    act3, cot3, hid, mid, _, keep, send = call(
        outer_kernel,
        "grad_two",
        [wide, wide, high, flat, turned] + parts,
        [lat_near, lat_far, k_one, act3, cot3, hid, mid, mid_t],
        flops=flops,
        scratch=[part, term],
        aliases={3: 0, 4: 1, 5: 2, 6: 3, 7: 4},
    )
    turns = Turns()
    two = Summed(keep, send, factor)
    turns.start(two)

    lanes = -(-(rows + 2) // 16) * 16
    sides = ((2 * lanes, chans), BF16)

    def grad_hid_part(waits):
        return call(
            back_kernel,
            "grad_hid",
            [flat, turned, sides, sides],
            [*after([lat_near], *waits), lat_far, t_two, cot3, hid, mid],
            flops=flops,
            scratch=[part, pltpu.VMEM((4 * lanes, chans), F32)],
        )

    def grad_one_part(waits):
        return call(
            grad_one_kernel,
            "grad_one",
            parts,
            [*after([ghid_t], *waits), act3],
            flops=flops,
            scratch=[term],
        )

    ghid, ghid_t, side_near, side_far = turns.run(grad_hid_part)
    keep, send = turns.run(grad_one_part)
    one = Summed(keep, send, factor)
    turns.start(one)
    turns.finish(two)
    turns.start(two)
    side_near, side_far = after([side_near, side_far], *turns.last)
    got_near = lax.ppermute(side_near, "lon", near_lon)
    got_far = lax.ppermute(side_far, "lon", far_lon)
    turns.finish(one)
    turns.start(one)
    got_near, got_far = after([got_near, got_far], *turns.last)
    turns.last = [got_near, got_far]
    turns.finish(two)
    turns.start(two)

    results = [None, None]

    def piece(which, half, waits):
        count = rows // 2
        ins = [got_near, got_far, *after([(mid, ghid)[which]], *waits)]
        ins += [(k_two, t_one)[which], field, cot]
        (results[which],) = call(
            functools.partial(last_kernel, bool(which), half * count, count),
            ("field_out", "grad_in")[which],
            [((cells, chans), BF16, "hbm")],
            ins + ([in_hbm(results[which])] if half else []),
            flops=flops // 2,
            scratch=[
                pltpu.VMEM((2 * lanes, chans), F32),
                pltpu.VMEM(((count + 2) * cols, 3 * chans), BF16),
                pltpu.VMEM((count * cols, chans), BF16),
                sems,
            ],
            aliases={len(ins): 0} if half else None,
        )
        return [results[which]]

    def scaling(chain):
        return lambda waits: [chain.scale(*after(chain.sent, *waits), True)]

    work = [functools.partial(piece, which, half) for which in (0, 1) for half in (0, 1)]
    while one.steps:
        if work:
            turns.run(work.pop(0))
        for chain in (one, two):
            if chain.steps:
                turns.finish(chain)
                if chain.steps:
                    turns.start(chain)
                if chain.steps and chain.steps[0][0] == "last":
                    turns.run(scaling(chain))
    while work:
        turns.run(work.pop(0))
    shape = (3, 3, chans, chans)
    return (
        results[0].reshape(rows, cols, chans),
        results[1].reshape(rows, cols, chans),
        one.result.reshape(shape),
        two.result.reshape(shape),
    )


def solution(mesh):
    return jax.shard_map(
        shards,
        mesh=mesh,
        in_specs=(P("lat", "lon", None), P(), P(), P("lat", "lon", None)),
        out_specs=(P("lat", "lon", None), P("lat", "lon", None), P(), P()),
        check_vma=False,
    )
```

```python
import functools

import jax
import jax.numpy as jnp
from jax import lax
from jax.experimental import pallas as pl
from jax.experimental.pallas import tpu as pltpu
from jax.sharding import PartitionSpec as P

BOTH = ("lat", "lon")
F32, BF16 = jnp.float32, jnp.bfloat16


def kernel_call(body, name, outs, ins, flops=0, scratch=(), aliases=None, limit=24, flush=()):
    outs, ins, scratch, aliases = list(outs), list(ins), list(scratch), dict(aliases or {})
    counts = len(ins), len(outs), len(scratch)
    rows, given = [], []
    for array, buffer, row, total in flush:
        ins.append(array)
        rows.append((row, array.shape[0]))
        given.append(buffer is not None)
        outs.append(((total, array.shape[1]), array.dtype, "hbm"))
        if buffer is not None:
            aliases[len(ins)] = len(outs) - 1
            ins.append(in_hbm(buffer))
        scratch.append(pltpu.SemaphoreType.DMA)
    if flush:
        body = functools.partial(flushing_kernel, body, counts, rows, given)
    out_shape, out_specs, in_specs, arrays = [], [], [], []
    for shape, kind, *spot in outs:
        out_shape.append(pltpu.HBM(shape, kind) if spot else pltpu.VMEM(shape, kind))
        out_specs.append(pl.BlockSpec(memory_space=pltpu.HBM if spot else pltpu.VMEM))
    for x in ins:
        far = isinstance(x, tuple)
        arrays.append(x[0] if far else x)
        in_specs.append(pl.BlockSpec(memory_space=pltpu.HBM if far else pltpu.VMEM))
    moved = sum(x.size * x.dtype.itemsize for x in arrays)
    return pl.pallas_call(
        body,
        out_shape=out_shape,
        in_specs=in_specs,
        out_specs=out_specs,
        scratch_shapes=scratch,
        input_output_aliases=aliases,
        compiler_params=pltpu.CompilerParams(vmem_limit_bytes=limit << 20),
        cost_estimate=pl.CostEstimate(flops=flops, bytes_accessed=moved, transcendentals=0),
        name=name,
    )(*arrays)


def flushing_kernel(body, counts, rows, given, *refs):
    refs = list(refs)

    def take(count):
        taken = refs[:count]
        del refs[:count]
        return taken

    ins = take(counts[0])
    sources = []
    for has_buffer in given:
        sources.append(take(1 + has_buffer)[0])
    outs, buffers = take(counts[1]), take(len(rows))
    scratch, sems = take(counts[2]), take(len(rows))
    copies = [
        pltpu.make_async_copy(source, buffer.at[pl.ds(row, count), :], sem)
        for source, buffer, sem, (row, count) in zip(sources, buffers, sems, rows)
    ]
    for copy in copies:
        copy.start()
    body(*ins, *outs, *scratch)
    for copy in copies:
        copy.wait()


def in_hbm(x):
    return (pltpu.with_memory_space_constraint(x, pltpu.HBM),)


def sigmoid(value):
    return 1.0 / (1.0 + jnp.exp(-value))


def silu(value):
    return value / (1.0 + jnp.exp(-value))


def same(value):
    return value


def silu_grad(value):
    sig = sigmoid(value)
    return sig * (1.0 + value * (1.0 - sig))


def aligned(start, step):
    return pl.multiple_of(start, step)


def is_odd(axis):
    return lax.axis_index(axis) % 2 == 1


def put_shifted(out, start, x, cols, left=None, right=None):
    chans = x.shape[1]
    col = lax.broadcasted_iota(jnp.int32, x.shape, 0)
    before = pltpu.roll(x, 1, 0)
    after = pltpu.roll(x, cols - 1, 0)
    if left is not None:
        before = jnp.where(col == 0, left, before)
        after = jnp.where(col == cols - 1, right, after)
    where = pl.ds(start, cols)
    out[where, :chans] = before.astype(BF16)
    out[where, chans : 2 * chans] = x.astype(BF16)
    out[where, 2 * chans :] = after.astype(BF16)


def conv_rows(shifted, weights, start, count, cols):
    piece = jnp.concatenate([shifted[pl.ds(start + i * cols, count), :] for i in range(3)], axis=1)
    return jnp.dot(piece, weights[...], preferred_element_type=F32)


def ends_kernel(cols, field_hbm, cot_hbm, field, cot, near, far, lines, sems):
    rows = field.shape[0] // cols
    copies = [
        pltpu.make_async_copy(field_hbm, field, sems.at[0]),
        pltpu.make_async_copy(cot_hbm, cot, sems.at[1]),
    ]
    for copy in copies:
        copy.start()
    odd = is_odd("lon")
    half = 4 * rows
    for n, (copy, source) in enumerate(zip(copies, (field, cot))):
        copy.wait()
        for r in range(rows):
            first = source[r * cols : r * cols + 16, :].astype(F32)
            last = source[(r + 1) * cols - 16 : (r + 1) * cols, :].astype(F32)
            for k in range(2):
                at = (2 * n + k) * rows + r
                lines[at : at + 1, :] = jnp.where(odd, first[k : k + 1], last[14 + k : 15 + k])
                at += half
                lines[at : at + 1, :] = jnp.where(odd, last[14 + k : 15 + k], first[k : k + 1])
    near[...] = lines[:half, :].astype(BF16)
    far[...] = lines[half:, :].astype(BF16)


def prep_kernel(cols, field, cot, one_hbm, two_hbm, act3, cot3, k_one, k_two, t_one, t_two, sems):
    rows = field.shape[0] // cols
    chans = field.shape[1]
    copies = [
        pltpu.make_async_copy(one_hbm, k_one, sems.at[0]),
        pltpu.make_async_copy(two_hbm, k_two, sems.at[1]),
    ]
    for copy in copies:
        copy.start()

    def body(r, carry):
        at = aligned(r * cols, cols)
        to = aligned((r + 1) * cols, cols)
        put_shifted(act3, to, silu(field[pl.ds(at, cols), :].astype(F32)), cols)
        put_shifted(cot3, to, cot[pl.ds(at, cols), :].astype(F32), cols)
        return carry

    lax.fori_loop(0, rows, body, 0, unroll=2)
    for copy in copies:
        copy.wait()
    for tap in range(9):
        to = slice((8 - tap) * chans, (9 - tap) * chans)
        at = slice(tap * chans, (tap + 1) * chans)
        t_one[to, :] = k_one[at, :].T
        t_two[to, :] = k_two[at, :].T


def edge_kernel(cols, field, cot, near, far, send_near, send_far):
    rows = field.shape[0] // cols
    chans = field.shape[1]
    odd = is_odd("lon")
    odd_lat = lax.axis_index("lat") % 2
    low, high = near[...].astype(F32), far[...].astype(F32)
    left, right = jnp.where(odd, low, high), jnp.where(odd, high, low)
    for out, first in ((send_near, odd_lat), (send_far, 1 - odd_lat)):
        start = aligned((1 - first) * (rows - 2) * cols, cols)
        out[: 2 * cols, :] = field[pl.ds(start, 2 * cols), :]
        out[2 * cols : 4 * cols, :] = cot[pl.ds(start, 2 * cols), :]
        lines = []
        for n in range(2):
            for r in range(2):
                for side in (left, right):
                    for k in range(2):
                        base = (2 * n + k) * rows
                        top = side[base + r : base + r + 1]
                        bottom = side[base + rows - 2 + r : base + rows - 1 + r]
                        lines.append(jnp.where(first == 1, top, bottom))
        out[4 * cols :, :] = jnp.concatenate(lines, axis=0).astype(BF16)


def inner_kernel(
    cols, near, far, k_one, t_two, _a, _c, act3, cot3, hid, mid, ghid, turned, edges
):
    rows = near.shape[0] // 4
    chans = near.shape[1]
    odd = is_odd("lon")
    low, high = near[...].astype(F32), far[...].astype(F32)
    edges[: 4 * rows, :] = jnp.where(odd, low, high)
    edges[4 * rows :, :] = jnp.where(odd, high, low)
    line = lax.broadcasted_iota(jnp.int32, (16, chans), 0)

    def patch(r, carry):
        start = aligned((r + 1) * cols, cols)
        end = aligned((r + 2) * cols - 16, 16)
        for out, base, fix in ((act3, 0, silu), (cot3, 2 * rows, same)):
            left = fix(edges[pl.ds(base + rows + r, 1), :]).astype(BF16).astype(F32)
            right = fix(edges[pl.ds(base + 4 * rows + r, 1), :]).astype(BF16).astype(F32)
            old = out[pl.ds(start, 16), :chans].astype(F32)
            out[pl.ds(start, 16), :chans] = jnp.where(line == 0, left, old).astype(BF16)
            old = out[pl.ds(end, 16), 2 * chans :].astype(F32)
            out[pl.ds(end, 16), 2 * chans :] = jnp.where(line == 15, right, old).astype(BF16)
        return carry

    lax.fori_loop(0, rows, patch, 0, unroll=4)
    for r, count in row_blocks(1, rows - 1):
        to = pl.ds((r + 1) * cols, count * cols)
        got = conv_rows(act3, k_one, r * cols, count * cols, cols)
        hid[to, :] = got
        mid[to, :] = silu(got).astype(BF16)
    for r, count in row_blocks(1, rows - 1):
        to = pl.ds((r + 1) * cols, count * cols)
        got = conv_rows(cot3, t_two, r * cols, count * cols, cols)
        ghid[to, :] = (got * silu_grad(hid[to, :])).astype(BF16)
    own = slice(3 * cols, (rows - 1) * cols)
    turned[:, 2 * cols : (rows - 2) * cols] = mid[own, :].T


def row_blocks(first, end):
    count = -(-(end - first) // 3)
    return [(r, min(count, end - r)) for r in range(first, end, count)]


def halo_rows(near, far):
    odd = is_odd("lat")
    low, high = near[...].astype(F32), far[...].astype(F32)
    return jnp.where(odd, low, high), jnp.where(odd, high, low)


def put_halo(part, halos, n, cols, fix, source):
    rows = source.shape[0] // cols - 2
    for half, halo in enumerate(halos):
        base = half * 4 * cols
        inside = rows - 1 if half else 1
        own = slice(inside * cols, (inside + 2) * cols)
        part[base + (1 - half) * 2 * cols : base + (2 - half) * 2 * cols, :] = source[own, :]
        for r in range(2):
            x = fix(halo[(2 * n + r) * cols : (2 * n + r + 1) * cols])
            corner = 4 * cols + 8 * n + 4 * r
            left, right = fix(halo[corner + 1 : corner + 2]), fix(halo[corner + 2 : corner + 3])
            put_shifted(part, base + (half * 2 + r) * cols, x, cols, left, right)


def edge_mask(half, cols, shape):
    lat = lax.axis_index("lat")
    there = lat < lax.axis_size("lat") - 1 if half else lat > 0
    line = lax.broadcasted_iota(jnp.int32, shape, 0)
    inner = line < cols if half else line >= cols
    return jnp.logical_or(inner, there)


def outer_kernel(
    cols, near, far, k_one, _a, _c, _h, _m, _t,
    act3, cot3, hid, mid, turned, keep, send, part,
):
    chans = mid.shape[1]
    rows = mid.shape[0] // cols - 2
    halos = halo_rows(near, far)
    put_halo(part, halos, 1, cols, same, cot3)
    cot3[:cols, :] = part[cols : 2 * cols, :]
    cot3[(rows + 1) * cols :, :] = part[6 * cols : 7 * cols, :]
    put_halo(part, halos, 0, cols, silu, act3)
    act3[:cols, :] = part[cols : 2 * cols, :]
    act3[(rows + 1) * cols :, :] = part[6 * cols : 7 * cols, :]
    for half in range(2):
        to = half * rows * cols
        got = conv_rows(part, k_one, half * 4 * cols, 2 * cols, cols)
        hid[to : to + 2 * cols, :] = got
        value = jnp.where(edge_mask(half, cols, got.shape), silu(got), 0.0)
        mid[to : to + 2 * cols, :] = value.astype(BF16)
    turned[:, : 2 * cols] = mid[cols : 3 * cols, :].T
    turned[:, (rows - 2) * cols :] = mid[(rows - 1) * cols : (rows + 1) * cols, :].T
    own = core_order(turned)
    half = chans // 2
    for i in range(3):
        got = jnp.dot(own, cot3[i * cols : (i + rows) * cols, :], preferred_element_type=F32)
        for j in range(3):
            tap = (2 - i) * 3 + 2 - j
            to, at = slice(tap * half, (tap + 1) * half), slice(j * chans, (j + 1) * chans)
            keep[to, :] = got[:half, at]
            send[to, :] = got[half:, at].astype(BF16)


def core_order(turned):
    half = turned.shape[0] // 2
    bit = lax.axis_index("lon") % 2
    mine, other = (pl.ds(aligned(x * half, 16), half) for x in (bit, 1 - bit))
    return jnp.concatenate([turned[mine, :], turned[other, :]], axis=0)


def grad_one_kernel(cols, near, far, t_two, cot3, act3, hid, _g, ghid, keep, send, turned, part):
    chans, cells = turned.shape
    rows = cells // cols
    put_halo(part, halo_rows(near, far), 1, cols, same, cot3)
    for half in range(2):
        to = slice(half * rows * cols, half * rows * cols + 2 * cols)
        got = conv_rows(part, t_two, half * 4 * cols, 2 * cols, cols)
        value = jnp.where(edge_mask(half, cols, got.shape), got * silu_grad(hid[to, :]), 0.0)
        ghid[to, :] = value.astype(BF16)
    turned[...] = ghid[cols : (rows + 1) * cols, :].T
    own = core_order(turned)
    half = chans // 2
    for i in range(3):
        got = jnp.dot(own, act3[i * cols : i * cols + cells, :], preferred_element_type=F32)
        for j in range(3):
            tap = i * 3 + j
            to, at = slice(tap * chans, (tap + 1) * chans), slice(j * chans, (j + 1) * chans)
            keep[to, :] = got[:half, at].T
            send[to, :] = got[half:, at].T.astype(BF16)


def rim_kernel(cols, own_near, own_far, near, far, lat_near, lat_far, k_one, t_two, mid, ghid):
    rows = near.shape[0] // 4
    chans = near.shape[1]
    lanes = mid.shape[0] // 2
    odd = is_odd("lon")
    pairs = [[x[...].astype(F32) for x in pair] for pair in ((own_far, own_near), (near, far))]
    (first, last), (left, right) = [
        (jnp.where(odd, b, a), jnp.where(odd, a, b)) for a, b in (pairs[0], pairs[1][::-1])
    ]
    halos = halo_rows(lat_near, lat_far)
    lat = lax.axis_index("lat")
    line = lax.broadcasted_iota(jnp.int32, (2 * lanes, chans), 0) % lanes
    inside = jnp.logical_and(
        jnp.logical_or(line > 0, lat > 0),
        jnp.logical_or(line <= rows, lat < lax.axis_size("lat") - 1),
    )

    def column(n, source, k, spot, fix):
        ends = []
        for halo in halos:
            for r in range(2):
                at = spot(n, r)
                ends.append(halo[at : at + 1])
        base = (2 * n + k) * rows
        filler = jnp.zeros((lanes - rows - 4, chans), F32)
        lines = [*ends[:2], source[base : base + rows], *ends[2:], filler]
        return fix(jnp.concatenate(lines, axis=0))

    def corner(k):
        return lambda n, r: 4 * cols + 8 * n + 4 * r + k

    def main(col):
        return lambda n, r: (2 * n + r) * cols + col

    results = []
    for n, (fix, weights) in enumerate(((silu, k_one), (same, t_two))):
        sides = []
        for spots in (
            ((left, 0, corner(0)), (left, 1, corner(1)), (first, 0, main(0))),
            ((last, 1, main(cols - 1)), (right, 0, corner(2)), (right, 1, corner(3))),
        ):
            three = jnp.concatenate(
                [column(n, source, k, spot, fix) for source, k, spot in spots], axis=1
            )
            nine = [three, pltpu.roll(three, lanes - 1, 0), pltpu.roll(three, lanes - 2, 0)]
            sides.append(jnp.concatenate(nine, axis=1))
        both = jnp.concatenate(sides, axis=0).astype(BF16)
        results.append(jnp.dot(both, weights[...], preferred_element_type=F32))
    hid, gmid = results
    mid[...] = jnp.where(inside, silu(hid), 0.0)
    ghid[...] = jnp.where(inside, gmid * silu_grad(hid), 0.0)


def last_kernel(backward, first, count, cols, edges, value, weights, field, cot, *rest):
    out, shifted = rest
    lanes = edges.shape[0] // 2

    def body(r, carry):
        x = value[pl.ds(aligned((first + r) * cols, cols), cols), :].astype(F32)
        left, right = edges[pl.ds(first + r, 1), :], edges[pl.ds(lanes + first + r, 1), :]
        put_shifted(shifted, aligned(r * cols, cols), x, cols, left, right)
        return carry

    lax.fori_loop(0, count + 2, body, 0, unroll=2)
    step = max(count // 2, 1)
    for r in range(0, count, step):
        at = slice((first + r) * cols, (first + r + step) * cols)
        to = slice(r * cols, (r + step) * cols)
        got = conv_rows(shifted, weights, r * cols, step * cols, cols)
        x = field[at, :].astype(F32)
        if backward:
            out[to, :] = (cot[at, :].astype(F32) + got * silu_grad(x)).astype(BF16)
        else:
            out[to, :] = (x + got).astype(BF16)


def place():
    return lax.axis_index("lat"), lax.axis_index("lon") % 2


def partner(n):
    lat, odd = place()
    even_mask, odd_mask = group_masks(lax.axis_size("lat"))[n]
    return lat ^ jnp.where(odd == 1, odd_mask, even_mask)


def chunk(index, rows):
    return pl.ds(aligned(index * rows, 16), rows)


def spread_kernel(keep, got, own, *sends):
    rows = own.shape[0]
    at = chunk(place()[0], rows)
    own[...] = keep[at, :] + got[at, :].astype(F32)
    for n, send in enumerate(sends):
        at = chunk(partner(n), rows)
        send[...] = (keep[at, :] + got[at, :].astype(F32)).astype(BF16)


def add_round_kernel(own, *rest):
    out = rest[-1]
    total = own[...].astype(F32)
    for got in rest[:-1]:
        total = total + got[...].astype(F32)
    out[...] = total.astype(BF16)


def join_kernel(value, *rest):
    out = rest[-1]
    rows = value.shape[0]
    out[chunk(place()[0], rows), :] = value[...]
    for n, got in enumerate(rest[:-1]):
        out[chunk(partner(n), rows), :] = got[...]


def scale_kernel(factor, own, got, out):
    half = out.shape[1] // 2
    bit = lax.axis_index("lon") % 2
    for tap in range(9):
        at = slice(tap * half, (tap + 1) * half)
        for x, which in ((own, bit), (got, 1 - bit)):
            to = pl.ds(aligned((2 * tap + which) * half, 16), half)
            out[to, :] = x[at, :].astype(F32) * factor


def final_kernel(factor, own, value, *rest):
    out, scaled, sems = rest[-3:]
    rows, half = value.shape
    count = rows // sems.shape[0]
    bit = lax.axis_index("lon") % 2
    lanes = pl.ds(aligned((bit if own else 1 - bit) * half, half), half)
    copies = []
    for n in range(sems.shape[0]):
        at = pl.ds(n * count, count)
        scaled[at, :] = value[at, :].astype(F32) * factor
        copies.append(pltpu.make_async_copy(scaled.at[at, :], out.at[at, lanes], sems.at[n]))
        copies[-1].start()
    for copy in copies:
        copy.wait()


def paired(count, offset, periodic):
    pairs = []
    for low in range(offset, count, 2):
        high = low + 1
        if high == count:
            if not periodic:
                continue
            high = 0
        pairs += [(low, high), (high, low)]
    return pairs


def log2(count):
    assert count & (count - 1) == 0
    return count.bit_length() - 1


def reversed_bits(value, width):
    return int(format(value, f"0{width}b")[::-1], 2)


def group_masks(count):
    return [(k, reversed_bits(k, log2(count))) for k in range(1, count)]


def flat_pairs(lat_count, lon_count, move):
    pairs = []
    for lat in range(lat_count):
        for lon in range(lon_count):
            to_lat, to_lon = move(lat, lon)
            pairs.append((lat * lon_count + lon, to_lat * lon_count + to_lon))
    return pairs


def after(values, *others):
    return list(lax.optimization_barrier((*values, *others)))[: len(values)]


class Summed:
    def __init__(self, keep, send, factor):
        lat_count, lon_count = lax.axis_size("lat"), lax.axis_size("lon")
        self.keep, self.sent, self.factor, self.result = keep, [send], factor, None
        core = flat_pairs(lat_count, lon_count, lambda lat, lon: (lat, lon ^ 1))
        group = [
            flat_pairs(
                lat_count, lon_count, lambda lat, lon, m=m: (lat ^ (m[1] if lon & 1 else m[0]), lon)
            )
            for m in group_masks(lat_count)
        ]
        width = log2(lon_count) - 1
        line = [
            flat_pairs(
                lat_count,
                lon_count,
                lambda lat, lon, n=n: (lat, lon ^ (2 << (width - 1 - n if lon & 1 else n))),
            )
            for n in range(width)
        ]
        self.steps = [("core", [core]), ("lat", group)]
        self.steps += [("lon", [pairs]) for pairs in line]
        self.steps += [("join", group), ("last", [core])]

    def start(self):
        kind, pairs = self.steps[0]
        sent = self.sent if kind == "lat" else self.sent * len(pairs)
        self.got = [lax.ppermute(x, BOTH, p) for x, p in zip(sent, pairs)]

    def finish(self):
        kind = self.steps.pop(0)[0]
        got, (rows, chans) = self.got, self.keep.shape
        if kind == "core":
            count = lax.axis_size("lat")
            piece = rows // count
            assert piece % 16 == 0
            outs = [((piece, chans), F32)] + [((piece, chans), BF16)] * (count - 1)
            self.keep, *self.sent = kernel_call(
                spread_kernel, "spread", outs, [self.keep, *got], limit=16
            )
        elif kind == "join":
            outs = [((rows * lax.axis_size("lat"), chans), BF16)]
            self.sent = kernel_call(join_kernel, "join", outs, [*self.sent, *got], limit=16)
        elif kind == "last" and self.result is None:
            outs = [((2 * rows * lax.axis_size("lat"), chans), F32)]
            body = functools.partial(scale_kernel, self.factor)
            (self.result,) = kernel_call(body, "scaled", outs, [*self.sent, *got], limit=16)
            self.sent = [self.result]
        elif kind == "last":
            self.sent = self.scale(got[0], False)
        else:
            mine = self.keep if kind == "lat" else self.sent[0]
            outs = [((rows, chans), BF16)]
            self.sent = kernel_call(add_round_kernel, "add", outs, [mine, *got], limit=16)

    def scale(self, value, own, flush=()):
        rows, chans = value.shape
        ins = [value] if own else [value, in_hbm(self.result)]
        self.result, *buffers = kernel_call(
            functools.partial(final_kernel, self.factor, own),
            "scaled",
            [((rows, 2 * chans), F32, "hbm")],
            ins,
            scratch=[pltpu.VMEM((rows, chans), F32), pltpu.SemaphoreType.DMA((4,))],
            aliases=None if own else {1: 0},
            limit=16,
            flush=flush,
        )
        return [self.result, *buffers]


class Turns:
    def __init__(self):
        self.last = []

    def run(self, work):
        result = work(self.last)
        self.last = list(result)
        return result

    def start(self, chain):
        chain.sent = after(chain.sent, *self.last)
        self.last = list(chain.sent)
        chain.start()

    def finish(self, chain):
        chain.got = after(chain.got, *self.last)
        chain.finish()
        self.last = list(chain.sent)


def shards(field_in, kernel_one, kernel_two, cotangent):
    rows, cols, chans = field_in.shape
    cells, tall = rows * cols, (rows + 2) * cols
    lat_count, lon_count = lax.axis_size("lat"), lax.axis_size("lon")
    factor = float(rows * lat_count * cols * lon_count) ** (-0.5)
    flops = 2 * cells * 9 * chans * chans
    sems = pltpu.SemaphoreType.DMA((2,))

    def call(body, *args, **kwargs):
        return kernel_call(functools.partial(body, cols), *args, **kwargs)

    near_lon, far_lon = paired(lon_count, 0, True), paired(lon_count, 1, True)
    near_lat, far_lat = paired(lat_count, 0, False), paired(lat_count, 1, False)

    tile = ((cells, chans), BF16)
    line = ((4 * rows, chans), BF16)
    field, cot, near, far = call(
        ends_kernel,
        "ends",
        [tile, tile, line, line],
        [in_hbm(field_in.reshape(cells, chans)), in_hbm(cotangent.reshape(cells, chans))],
        scratch=[pltpu.VMEM((8 * rows, chans), F32), sems],
    )
    lon_near = lax.ppermute(near, "lon", near_lon)
    lon_far = lax.ppermute(far, "lon", far_lon)
    wide = ((tall, 3 * chans), BF16)
    square = ((9 * chans, chans), BF16)
    act3, cot3, k_one, k_two, t_one, t_two = call(
        prep_kernel,
        "prep",
        [wide, wide, square, square, square, square],
        [field, cot] + [in_hbm(k.reshape(9 * chans, chans)) for k in (kernel_one, kernel_two)],
        flops=flops,
        scratch=[sems],
    )

    strip = ((4 * cols + 16, chans), BF16)
    send_near, send_far = call(
        edge_kernel, "edges", [strip, strip], [field, cot, *after([lon_near, lon_far], act3)]
    )
    lat_near = lax.ppermute(send_near, "lat", near_lat)
    lat_far = lax.ppermute(send_far, "lat", far_lat)

    high = ((tall, chans), F32)
    flat = ((tall, chans), BF16)
    turned = ((chans, cells), BF16)
    act3, cot3, hid, mid, ghid, mid_t = call(
        inner_kernel,
        "inner_rows",
        [wide, wide, high, flat, flat, turned],
        [lon_near, lon_far, k_one, t_two, *after([act3], send_near, send_far), cot3],
        flops=2 * flops,
        scratch=[pltpu.VMEM((8 * rows, chans), F32)],
        aliases={4: 0, 5: 1},
    )
    half = (9 * chans // 2, chans)
    parts = [(half, F32), (half, BF16)]
    part = pltpu.VMEM((8 * cols, 3 * chans), BF16)
    act3, cot3, hid, mid, _, keep, send = call(
        outer_kernel,
        "grad_two",
        [wide, wide, high, flat, turned] + parts,
        [lat_near, lat_far, k_one, act3, cot3, hid, mid, mid_t],
        flops=flops,
        scratch=[part],
        aliases={3: 0, 4: 1, 5: 2, 6: 3, 7: 4},
    )
    turns = Turns()
    two = Summed(keep, send, factor)
    turns.start(two)

    lanes = -(-(rows + 4) // 8) * 8
    rim = ((2 * lanes, chans), F32)

    def rim_part(waits):
        return call(
            rim_kernel,
            "rim",
            [rim, rim],
            [near, far, *after([lon_near, lon_far], *waits), lat_near, lat_far, k_one, t_two],
            flops=flops // 16,
        )

    def grad_one_part(waits):
        return call(
            grad_one_kernel,
            "grad_one",
            [flat] + [((9 * chans, chans // 2), kind) for kind in (F32, BF16)],
            [*after([lat_near], *waits), lat_far, t_two, cot3, act3, hid, ghid],
            flops=flops,
            scratch=[pltpu.VMEM((chans, cells), BF16), part],
            aliases={6: 0},
        )

    ghid, keep, send = turns.run(grad_one_part)
    one = Summed(keep, send, factor)
    turns.start(one)
    turns.finish(two)
    turns.start(two)
    turns.finish(one)
    turns.start(one)
    rims = turns.run(rim_part)
    turns.finish(two)
    turns.start(two)

    results = [None, None]
    waiting = []

    def flushed(buffers):
        for (which, _, _), buffer in zip(waiting, buffers):
            results[which] = buffer
        waiting.clear()

    def flushes():
        return [(x, results[which], row, cells) for which, x, row in waiting]

    def piece(which, half, waits):
        count = rows // 2
        result, *buffers = call(
            functools.partial(last_kernel, bool(which), half * count, count),
            ("field_out", "grad_in")[which],
            [((count * cols, chans), BF16)],
            [rims[which], *after([(mid, ghid)[which]], *waits)]
            + [(k_two, t_one)[which], field, cot],
            flops=flops // 2,
            scratch=[pltpu.VMEM(((count + 2) * cols, 3 * chans), BF16)],
            flush=flushes(),
        )
        flushed(buffers)
        waiting.append((which, result, half * count * cols))
        return [result, *buffers]

    def own_half(waits):
        more = [(two.result, None, 0, 9 * chans)]
        value = after(one.sent, *waits)[0]
        result, *buffers = one.scale(value, True, flushes() + more)
        two.result = buffers.pop()
        flushed(buffers)
        return [result, *buffers, two.result]

    work = [functools.partial(piece, which, half) for which in (0, 1) for half in (0, 1)]
    for turn in (0, one, two, 1, one, two, 2, one, two, 3):
        if isinstance(turn, int):
            turns.run(work[turn])
        elif turn.steps:
            turns.finish(turn)
            if turn.steps:
                turns.start(turn)
    while len(one.steps) > 1 or two.steps:
        for chain in (one, two):
            if len(chain.steps) > 1 or chain is two and chain.steps:
                turns.finish(chain)
                if chain.steps:
                    turns.start(chain)
    turns.run(own_half)
    turns.finish(one)
    shape = (3, 3, chans, chans)
    return (
        results[0].reshape(rows, cols, chans),
        results[1].reshape(rows, cols, chans),
        one.result.reshape(shape),
        two.result.reshape(shape),
    )


def solution(mesh):
    return jax.shard_map(
        shards,
        mesh=mesh,
        in_specs=(P("lat", "lon", None), P(), P(), P("lat", "lon", None)),
        out_specs=(P("lat", "lon", None), P("lat", "lon", None), P(), P()),
        check_vma=False,
    )
```

```python
import functools

import jax
import jax.numpy as jnp
from jax import lax
from jax.experimental import pallas as pl
from jax.experimental.pallas import tpu as pltpu
from jax.sharding import PartitionSpec as P

BOTH = ("lat", "lon")
F32, BF16 = jnp.float32, jnp.bfloat16


def kernel_call(body, name, outs, ins, flops=0, scratch=(), aliases=None, limit=24, flush=()):
    outs, ins, scratch, aliases = list(outs), list(ins), list(scratch), dict(aliases or {})
    counts = len(ins), len(outs), len(scratch)
    rows, given = [], []
    for array, buffer, row, total in flush:
        ins.append(array)
        rows.append((row, array.shape[0]))
        given.append(buffer is not None)
        outs.append(((total, array.shape[1]), array.dtype, "hbm"))
        if buffer is not None:
            aliases[len(ins)] = len(outs) - 1
            ins.append(in_hbm(buffer))
        scratch.append(pltpu.SemaphoreType.DMA)
    if flush:
        body = functools.partial(flushing_kernel, body, counts, rows, given)
    out_shape, out_specs, in_specs, arrays = [], [], [], []
    for shape, kind, *spot in outs:
        out_shape.append(pltpu.HBM(shape, kind) if spot else pltpu.VMEM(shape, kind))
        out_specs.append(pl.BlockSpec(memory_space=pltpu.HBM if spot else pltpu.VMEM))
    for x in ins:
        far = isinstance(x, tuple)
        arrays.append(x[0] if far else x)
        in_specs.append(pl.BlockSpec(memory_space=pltpu.HBM if far else pltpu.VMEM))
    moved = sum(x.size * x.dtype.itemsize for x in arrays)
    return pl.pallas_call(
        body,
        out_shape=out_shape,
        in_specs=in_specs,
        out_specs=out_specs,
        scratch_shapes=scratch,
        input_output_aliases=aliases,
        compiler_params=pltpu.CompilerParams(vmem_limit_bytes=limit << 20),
        cost_estimate=pl.CostEstimate(flops=flops, bytes_accessed=moved, transcendentals=0),
        name=name,
    )(*arrays)


def flushing_kernel(body, counts, rows, given, *refs):
    refs = list(refs)

    def take(count):
        taken = refs[:count]
        del refs[:count]
        return taken

    ins = take(counts[0])
    sources = []
    for has_buffer in given:
        sources.append(take(1 + has_buffer)[0])
    outs, buffers = take(counts[1]), take(len(rows))
    scratch, sems = take(counts[2]), take(len(rows))
    copies = [
        pltpu.make_async_copy(source, buffer.at[pl.ds(row, count), :], sem)
        for source, buffer, sem, (row, count) in zip(sources, buffers, sems, rows)
    ]
    for copy in copies:
        copy.start()
    body(*ins, *outs, *scratch)
    for copy in copies:
        copy.wait()


def in_hbm(x):
    return (pltpu.with_memory_space_constraint(x, pltpu.HBM),)


def sigmoid(value):
    return 1.0 / (1.0 + jnp.exp(-value))


def silu(value):
    return value / (1.0 + jnp.exp(-value))


def same(value):
    return value


def silu_grad(value):
    sig = sigmoid(value)
    return sig * (1.0 + value * (1.0 - sig))


def aligned(start, step):
    return pl.multiple_of(start, step)


def is_odd(axis):
    return lax.axis_index(axis) % 2 == 1


def put_shifted(out, start, x, cols, left=None, right=None):
    chans = x.shape[1]
    col = lax.broadcasted_iota(jnp.int32, x.shape, 0)
    before = pltpu.roll(x, 1, 0)
    after = pltpu.roll(x, cols - 1, 0)
    if left is not None:
        before = jnp.where(col == 0, left, before)
        after = jnp.where(col == cols - 1, right, after)
    where = pl.ds(start, cols)
    out[where, :chans] = before.astype(BF16)
    out[where, chans : 2 * chans] = x.astype(BF16)
    out[where, 2 * chans :] = after.astype(BF16)


def conv_rows(shifted, weights, start, count, cols):
    piece = jnp.concatenate([shifted[pl.ds(start + i * cols, count), :] for i in range(3)], axis=1)
    return jnp.dot(piece, weights[...], preferred_element_type=F32)


def ends_kernel(cols, field_hbm, cot_hbm, field, cot, near, far, lines, sems):
    rows = field.shape[0] // cols
    copies = [
        pltpu.make_async_copy(field_hbm, field, sems.at[0]),
        pltpu.make_async_copy(cot_hbm, cot, sems.at[1]),
    ]
    for copy in copies:
        copy.start()
    odd = is_odd("lon")
    half = 4 * rows
    for n, (copy, source) in enumerate(zip(copies, (field, cot))):
        copy.wait()
        for r in range(rows):
            first = source[r * cols : r * cols + 16, :].astype(F32)
            last = source[(r + 1) * cols - 16 : (r + 1) * cols, :].astype(F32)
            for k in range(2):
                at = (2 * n + k) * rows + r
                lines[at : at + 1, :] = jnp.where(odd, first[k : k + 1], last[14 + k : 15 + k])
                at += half
                lines[at : at + 1, :] = jnp.where(odd, last[14 + k : 15 + k], first[k : k + 1])
    near[...] = lines[:half, :].astype(BF16)
    far[...] = lines[half:, :].astype(BF16)


def prep_kernel(cols, field, cot, one_hbm, two_hbm, act3, cot3, k_one, k_two, t_one, t_two, sems):
    rows = field.shape[0] // cols
    chans = field.shape[1]
    copies = [
        pltpu.make_async_copy(one_hbm, k_one, sems.at[0]),
        pltpu.make_async_copy(two_hbm, k_two, sems.at[1]),
    ]
    for copy in copies:
        copy.start()

    def body(r, carry):
        at = aligned(r * cols, cols)
        to = aligned((r + 1) * cols, cols)
        put_shifted(act3, to, silu(field[pl.ds(at, cols), :].astype(F32)), cols)
        put_shifted(cot3, to, cot[pl.ds(at, cols), :].astype(F32), cols)
        return carry

    lax.fori_loop(0, rows, body, 0, unroll=4)
    for copy in copies:
        copy.wait()
    for tap in range(9):
        to = slice((8 - tap) * chans, (9 - tap) * chans)
        at = slice(tap * chans, (tap + 1) * chans)
        t_one[to, :] = k_one[at, :].T
        t_two[to, :] = k_two[at, :].T


def edge_kernel(cols, field, cot, near, far, send_near, send_far):
    rows = field.shape[0] // cols
    chans = field.shape[1]
    odd = is_odd("lon")
    odd_lat = lax.axis_index("lat") % 2
    low, high = near[...].astype(F32), far[...].astype(F32)
    left, right = jnp.where(odd, low, high), jnp.where(odd, high, low)
    for out, first in ((send_near, odd_lat), (send_far, 1 - odd_lat)):
        start = aligned((1 - first) * (rows - 2) * cols, cols)
        out[: 2 * cols, :] = field[pl.ds(start, 2 * cols), :]
        out[2 * cols : 4 * cols, :] = cot[pl.ds(start, 2 * cols), :]
        lines = []
        for n in range(2):
            for r in range(2):
                for side in (left, right):
                    for k in range(2):
                        base = (2 * n + k) * rows
                        top = side[base + r : base + r + 1]
                        bottom = side[base + rows - 2 + r : base + rows - 1 + r]
                        lines.append(jnp.where(first == 1, top, bottom))
        out[4 * cols :, :] = jnp.concatenate(lines, axis=0).astype(BF16)


def inner_kernel(
    cols, near, far, k_one, t_two, _a, _c, act3, cot3, hid, mid, ghid, turned, edges
):
    rows = near.shape[0] // 4
    chans = near.shape[1]
    odd = is_odd("lon")
    low, high = near[...].astype(F32), far[...].astype(F32)
    edges[: 4 * rows, :] = jnp.where(odd, low, high)
    edges[4 * rows :, :] = jnp.where(odd, high, low)
    line = lax.broadcasted_iota(jnp.int32, (16, chans), 0)

    def patch(r, carry):
        start = aligned((r + 1) * cols, cols)
        end = aligned((r + 2) * cols - 16, 16)
        for out, base, fix in ((act3, 0, silu), (cot3, 2 * rows, same)):
            left = fix(edges[pl.ds(base + rows + r, 1), :]).astype(BF16).astype(F32)
            right = fix(edges[pl.ds(base + 4 * rows + r, 1), :]).astype(BF16).astype(F32)
            old = out[pl.ds(start, 16), :chans].astype(F32)
            out[pl.ds(start, 16), :chans] = jnp.where(line == 0, left, old).astype(BF16)
            old = out[pl.ds(end, 16), 2 * chans :].astype(F32)
            out[pl.ds(end, 16), 2 * chans :] = jnp.where(line == 15, right, old).astype(BF16)
        return carry

    lax.fori_loop(0, rows, patch, 0, unroll=4)
    for r, count in row_blocks(1, rows - 1):
        to = pl.ds((r + 1) * cols, count * cols)
        got = conv_rows(act3, k_one, r * cols, count * cols, cols)
        hid[to, :] = got
        mid[to, :] = silu(got).astype(BF16)
    for r, count in row_blocks(1, rows - 1):
        to = pl.ds((r + 1) * cols, count * cols)
        got = conv_rows(cot3, t_two, r * cols, count * cols, cols)
        ghid[to, :] = (got * silu_grad(hid[to, :])).astype(BF16)
    own = slice(3 * cols, (rows - 1) * cols)
    turned[:, 2 * cols : (rows - 2) * cols] = mid[own, :].T


def row_blocks(first, end):
    count = -(-(end - first) // 3)
    return [(r, min(count, end - r)) for r in range(first, end, count)]


def halo_rows(near, far):
    odd = is_odd("lat")
    low, high = near[...].astype(F32), far[...].astype(F32)
    return jnp.where(odd, low, high), jnp.where(odd, high, low)


def put_halo(part, halos, n, cols, fix, source):
    rows = source.shape[0] // cols - 2
    for half, halo in enumerate(halos):
        base = half * 4 * cols
        inside = rows - 1 if half else 1
        own = slice(inside * cols, (inside + 2) * cols)
        part[base + (1 - half) * 2 * cols : base + (2 - half) * 2 * cols, :] = source[own, :]
        for r in range(2):
            x = fix(halo[(2 * n + r) * cols : (2 * n + r + 1) * cols])
            corner = 4 * cols + 8 * n + 4 * r
            left, right = fix(halo[corner + 1 : corner + 2]), fix(halo[corner + 2 : corner + 3])
            put_shifted(part, base + (half * 2 + r) * cols, x, cols, left, right)


def edge_mask(half, cols, shape):
    lat = lax.axis_index("lat")
    there = lat < lax.axis_size("lat") - 1 if half else lat > 0
    line = lax.broadcasted_iota(jnp.int32, shape, 0)
    inner = line < cols if half else line >= cols
    return jnp.logical_or(inner, there)


def outer_kernel(
    cols, near, far, k_one, _a, _c, _h, _m, _t,
    act3, cot3, hid, mid, turned, keep, send, part,
):
    chans = mid.shape[1]
    rows = mid.shape[0] // cols - 2
    halos = halo_rows(near, far)
    put_halo(part, halos, 1, cols, same, cot3)
    cot3[:cols, :] = part[cols : 2 * cols, :]
    cot3[(rows + 1) * cols :, :] = part[6 * cols : 7 * cols, :]
    put_halo(part, halos, 0, cols, silu, act3)
    act3[:cols, :] = part[cols : 2 * cols, :]
    act3[(rows + 1) * cols :, :] = part[6 * cols : 7 * cols, :]
    for half in range(2):
        to = half * rows * cols
        got = conv_rows(part, k_one, half * 4 * cols, 2 * cols, cols)
        hid[to : to + 2 * cols, :] = got
        value = jnp.where(edge_mask(half, cols, got.shape), silu(got), 0.0)
        mid[to : to + 2 * cols, :] = value.astype(BF16)
    turned[:, : 2 * cols] = mid[cols : 3 * cols, :].T
    turned[:, (rows - 2) * cols :] = mid[(rows - 1) * cols : (rows + 1) * cols, :].T
    own = core_order(turned)
    half = chans // 2
    for i in range(3):
        got = jnp.dot(own, cot3[i * cols : (i + rows) * cols, :], preferred_element_type=F32)
        for j in range(3):
            tap = (2 - i) * 3 + 2 - j
            to, at = slice(tap * half, (tap + 1) * half), slice(j * chans, (j + 1) * chans)
            keep[to, :] = got[:half, at]
            send[to, :] = got[half:, at].astype(BF16)


def core_order(turned):
    half = turned.shape[0] // 2
    bit = lax.axis_index("lon") % 2
    mine, other = (pl.ds(aligned(x * half, 16), half) for x in (bit, 1 - bit))
    return jnp.concatenate([turned[mine, :], turned[other, :]], axis=0)


def grad_one_kernel(cols, near, far, t_two, cot3, act3, hid, _g, ghid, keep, send, turned, part):
    chans, cells = turned.shape
    rows = cells // cols
    put_halo(part, halo_rows(near, far), 1, cols, same, cot3)
    for half in range(2):
        to = slice(half * rows * cols, half * rows * cols + 2 * cols)
        got = conv_rows(part, t_two, half * 4 * cols, 2 * cols, cols)
        value = jnp.where(edge_mask(half, cols, got.shape), got * silu_grad(hid[to, :]), 0.0)
        ghid[to, :] = value.astype(BF16)
    turned[...] = ghid[cols : (rows + 1) * cols, :].T
    own = core_order(turned)
    half = chans // 2
    for i in range(3):
        got = jnp.dot(own, act3[i * cols : i * cols + cells, :], preferred_element_type=F32)
        for j in range(3):
            tap = i * 3 + j
            to, at = slice(tap * chans, (tap + 1) * chans), slice(j * chans, (j + 1) * chans)
            keep[to, :] = got[:half, at].T
            send[to, :] = got[half:, at].T.astype(BF16)


def rim_kernel(cols, own_near, own_far, near, far, lat_near, lat_far, k_one, t_two, mid, ghid):
    rows = near.shape[0] // 4
    chans = near.shape[1]
    lanes = mid.shape[0] // 2
    odd = is_odd("lon")
    pairs = [[x[...].astype(F32) for x in pair] for pair in ((own_far, own_near), (near, far))]
    (first, last), (left, right) = [
        (jnp.where(odd, b, a), jnp.where(odd, a, b)) for a, b in (pairs[0], pairs[1][::-1])
    ]
    halos = halo_rows(lat_near, lat_far)
    lat = lax.axis_index("lat")
    line = lax.broadcasted_iota(jnp.int32, (2 * lanes, chans), 0) % lanes
    inside = jnp.logical_and(
        jnp.logical_or(line > 0, lat > 0),
        jnp.logical_or(line <= rows, lat < lax.axis_size("lat") - 1),
    )

    def column(n, source, k, spot, fix):
        ends = []
        for halo in halos:
            for r in range(2):
                at = spot(n, r)
                ends.append(halo[at : at + 1])
        base = (2 * n + k) * rows
        filler = jnp.zeros((lanes - rows - 4, chans), F32)
        lines = [*ends[:2], source[base : base + rows], *ends[2:], filler]
        return fix(jnp.concatenate(lines, axis=0))

    def corner(k):
        return lambda n, r: 4 * cols + 8 * n + 4 * r + k

    def main(col):
        return lambda n, r: (2 * n + r) * cols + col

    results = []
    for n, (fix, weights) in enumerate(((silu, k_one), (same, t_two))):
        sides = []
        for spots in (
            ((left, 0, corner(0)), (left, 1, corner(1)), (first, 0, main(0))),
            ((last, 1, main(cols - 1)), (right, 0, corner(2)), (right, 1, corner(3))),
        ):
            three = jnp.concatenate(
                [column(n, source, k, spot, fix) for source, k, spot in spots], axis=1
            )
            nine = [three, pltpu.roll(three, lanes - 1, 0), pltpu.roll(three, lanes - 2, 0)]
            sides.append(jnp.concatenate(nine, axis=1))
        both = jnp.concatenate(sides, axis=0).astype(BF16)
        results.append(jnp.dot(both, weights[...], preferred_element_type=F32))
    hid, gmid = results
    mid[...] = jnp.where(inside, silu(hid), 0.0)
    ghid[...] = jnp.where(inside, gmid * silu_grad(hid), 0.0)


def last_kernel(backward, first, count, cols, edges, value, weights, field, cot, *rest):
    out, shifted = rest
    lanes = edges.shape[0] // 2

    def body(r, carry):
        x = value[pl.ds(aligned((first + r) * cols, cols), cols), :].astype(F32)
        left, right = edges[pl.ds(first + r, 1), :], edges[pl.ds(lanes + first + r, 1), :]
        put_shifted(shifted, aligned(r * cols, cols), x, cols, left, right)
        return carry

    lax.fori_loop(0, count + 2, body, 0, unroll=2)
    step = max(count // 2, 1)
    for r in range(0, count, step):
        at = slice((first + r) * cols, (first + r + step) * cols)
        to = slice(r * cols, (r + step) * cols)
        got = conv_rows(shifted, weights, r * cols, step * cols, cols)
        x = field[at, :].astype(F32)
        if backward:
            out[to, :] = (cot[at, :].astype(F32) + got * silu_grad(x)).astype(BF16)
        else:
            out[to, :] = (x + got).astype(BF16)


def place():
    return lax.axis_index("lat"), lax.axis_index("lon") % 2


def partner(n):
    lat, odd = place()
    even_mask, odd_mask = group_masks(lax.axis_size("lat"))[n]
    return lat ^ jnp.where(odd == 1, odd_mask, even_mask)


def chunk(index, rows):
    return pl.ds(aligned(index * rows, 16), rows)


def spread_kernel(keep, got, own, *sends):
    rows = own.shape[0]
    at = chunk(place()[0], rows)
    own[...] = keep[at, :] + got[at, :].astype(F32)
    for n, send in enumerate(sends):
        at = chunk(partner(n), rows)
        send[...] = (keep[at, :] + got[at, :].astype(F32)).astype(BF16)


def add_round_kernel(own, *rest):
    out = rest[-1]
    total = own[...].astype(F32)
    for got in rest[:-1]:
        total = total + got[...].astype(F32)
    out[...] = total.astype(BF16)


def join_kernel(value, *rest):
    out = rest[-1]
    rows = value.shape[0]
    out[chunk(place()[0], rows), :] = value[...]
    for n, got in enumerate(rest[:-1]):
        out[chunk(partner(n), rows), :] = got[...]


def scale_kernel(factor, own, got, out):
    half = out.shape[1] // 2
    bit = lax.axis_index("lon") % 2
    for tap in range(9):
        at = slice(tap * half, (tap + 1) * half)
        for x, which in ((own, bit), (got, 1 - bit)):
            to = pl.ds(aligned((2 * tap + which) * half, 16), half)
            out[to, :] = x[at, :].astype(F32) * factor


def final_kernel(factor, own, value, *rest):
    out, scaled, sems = rest[-3:]
    rows, half = value.shape
    count = rows // sems.shape[0]
    bit = lax.axis_index("lon") % 2
    lanes = pl.ds(aligned((bit if own else 1 - bit) * half, half), half)
    copies = []
    for n in range(sems.shape[0]):
        at = pl.ds(n * count, count)
        scaled[at, :] = value[at, :].astype(F32) * factor
        copies.append(pltpu.make_async_copy(scaled.at[at, :], out.at[at, lanes], sems.at[n]))
        copies[-1].start()
    for copy in copies:
        copy.wait()


def paired(count, offset, periodic):
    pairs = []
    for low in range(offset, count, 2):
        high = low + 1
        if high == count:
            if not periodic:
                continue
            high = 0
        pairs += [(low, high), (high, low)]
    return pairs


def log2(count):
    assert count & (count - 1) == 0
    return count.bit_length() - 1


def reversed_bits(value, width):
    return int(format(value, f"0{width}b")[::-1], 2)


def group_masks(count):
    return [(k, reversed_bits(k, log2(count))) for k in range(1, count)]


def flat_pairs(lat_count, lon_count, move):
    pairs = []
    for lat in range(lat_count):
        for lon in range(lon_count):
            to_lat, to_lon = move(lat, lon)
            pairs.append((lat * lon_count + lon, to_lat * lon_count + to_lon))
    return pairs


def after(values, *others):
    return list(lax.optimization_barrier((*values, *others)))[: len(values)]


class Summed:
    def __init__(self, keep, send, factor):
        lat_count, lon_count = lax.axis_size("lat"), lax.axis_size("lon")
        self.keep, self.sent, self.factor, self.result = keep, [send], factor, None
        core = flat_pairs(lat_count, lon_count, lambda lat, lon: (lat, lon ^ 1))
        group = [
            flat_pairs(
                lat_count, lon_count, lambda lat, lon, m=m: (lat ^ (m[1] if lon & 1 else m[0]), lon)
            )
            for m in group_masks(lat_count)
        ]
        width = log2(lon_count) - 1
        line = [
            flat_pairs(
                lat_count,
                lon_count,
                lambda lat, lon, n=n: (lat, lon ^ (2 << (width - 1 - n if lon & 1 else n))),
            )
            for n in range(width)
        ]
        self.steps = [("core", [core]), ("lat", group)]
        self.steps += [("lon", [pairs]) for pairs in line]
        self.steps += [("join", group), ("last", [core])]

    def start(self):
        kind, pairs = self.steps[0]
        sent = self.sent if kind == "lat" else self.sent * len(pairs)
        self.got = [lax.ppermute(x, BOTH, p) for x, p in zip(sent, pairs)]

    def finish(self):
        kind = self.steps.pop(0)[0]
        got, (rows, chans) = self.got, self.keep.shape
        if kind == "core":
            count = lax.axis_size("lat")
            piece = rows // count
            assert piece % 16 == 0
            outs = [((piece, chans), F32)] + [((piece, chans), BF16)] * (count - 1)
            self.keep, *self.sent = kernel_call(
                spread_kernel, "spread", outs, [self.keep, *got], limit=16
            )
        elif kind == "join":
            outs = [((rows * lax.axis_size("lat"), chans), BF16)]
            self.sent = kernel_call(join_kernel, "join", outs, [*self.sent, *got], limit=16)
        elif kind == "last" and self.result is None:
            outs = [((2 * rows * lax.axis_size("lat"), chans), F32)]
            body = functools.partial(scale_kernel, self.factor)
            (self.result,) = kernel_call(body, "scaled", outs, [*self.sent, *got], limit=16)
            self.sent = [self.result]
        elif kind == "last":
            self.sent = self.scale(got[0], False)
        else:
            mine = self.keep if kind == "lat" else self.sent[0]
            outs = [((rows, chans), BF16)]
            self.sent = kernel_call(add_round_kernel, "add", outs, [mine, *got], limit=16)

    def scale(self, value, own, flush=()):
        rows, chans = value.shape
        ins = [value] if own else [value, in_hbm(self.result)]
        self.result, *buffers = kernel_call(
            functools.partial(final_kernel, self.factor, own),
            "scaled",
            [((rows, 2 * chans), F32, "hbm")],
            ins,
            scratch=[pltpu.VMEM((rows, chans), F32), pltpu.SemaphoreType.DMA((4,))],
            aliases=None if own else {1: 0},
            limit=16,
            flush=flush,
        )
        return [self.result, *buffers]


class Turns:
    def __init__(self):
        self.last = []

    def run(self, work):
        result = work(self.last)
        self.last = list(result)
        return result

    def start(self, chain):
        chain.sent = after(chain.sent, *self.last)
        self.last = list(chain.sent)
        chain.start()

    def finish(self, chain):
        chain.got = after(chain.got, *self.last)
        chain.finish()
        self.last = list(chain.sent)


def shards(field_in, kernel_one, kernel_two, cotangent):
    rows, cols, chans = field_in.shape
    cells, tall = rows * cols, (rows + 2) * cols
    lat_count, lon_count = lax.axis_size("lat"), lax.axis_size("lon")
    factor = float(rows * lat_count * cols * lon_count) ** (-0.5)
    flops = 2 * cells * 9 * chans * chans
    sems = pltpu.SemaphoreType.DMA((2,))

    def call(body, *args, **kwargs):
        return kernel_call(functools.partial(body, cols), *args, **kwargs)

    near_lon, far_lon = paired(lon_count, 0, True), paired(lon_count, 1, True)
    near_lat, far_lat = paired(lat_count, 0, False), paired(lat_count, 1, False)

    tile = ((cells, chans), BF16)
    line = ((4 * rows, chans), BF16)
    field, cot, near, far = call(
        ends_kernel,
        "ends",
        [tile, tile, line, line],
        [in_hbm(field_in.reshape(cells, chans)), in_hbm(cotangent.reshape(cells, chans))],
        scratch=[pltpu.VMEM((8 * rows, chans), F32), sems],
    )
    lon_far = lax.ppermute(far, "lon", far_lon)
    wide = ((tall, 3 * chans), BF16)
    square = ((9 * chans, chans), BF16)
    act3, cot3, k_one, k_two, t_one, t_two = call(
        prep_kernel,
        "prep",
        [wide, wide, square, square, square, square],
        [field, cot] + [in_hbm(k.reshape(9 * chans, chans)) for k in (kernel_one, kernel_two)],
        flops=flops,
        scratch=[sems],
    )

    lon_near = lax.ppermute(after([near], act3)[0], "lon", near_lon)

    strip = ((4 * cols + 16, chans), BF16)
    send_near, send_far = call(
        edge_kernel, "edges", [strip, strip], [field, cot, *after([lon_near, lon_far], act3)]
    )
    lat_near = lax.ppermute(send_near, "lat", near_lat)
    lat_far = lax.ppermute(send_far, "lat", far_lat)

    high = ((tall, chans), F32)
    flat = ((tall, chans), BF16)
    turned = ((chans, cells), BF16)
    act3, cot3, hid, mid, ghid, mid_t = call(
        inner_kernel,
        "inner_rows",
        [wide, wide, high, flat, flat, turned],
        [lon_near, lon_far, k_one, t_two, *after([act3], send_near, send_far), cot3],
        flops=2 * flops,
        scratch=[pltpu.VMEM((8 * rows, chans), F32)],
        aliases={4: 0, 5: 1},
    )
    half = (9 * chans // 2, chans)
    parts = [(half, F32), (half, BF16)]
    part = pltpu.VMEM((8 * cols, 3 * chans), BF16)
    act3, cot3, hid, mid, _, keep, send = call(
        outer_kernel,
        "grad_two",
        [wide, wide, high, flat, turned] + parts,
        [lat_near, lat_far, k_one, act3, cot3, hid, mid, mid_t],
        flops=flops,
        scratch=[part],
        aliases={3: 0, 4: 1, 5: 2, 6: 3, 7: 4},
    )
    turns = Turns()
    two = Summed(keep, send, factor)
    turns.start(two)

    lanes = -(-(rows + 4) // 8) * 8
    rim = ((2 * lanes, chans), F32)

    def rim_part(waits):
        return call(
            rim_kernel,
            "rim",
            [rim, rim],
            [near, far, *after([lon_near, lon_far], *waits), lat_near, lat_far, k_one, t_two],
            flops=flops // 16,
        )

    def grad_one_part(waits):
        return call(
            grad_one_kernel,
            "grad_one",
            [flat] + [((9 * chans, chans // 2), kind) for kind in (F32, BF16)],
            [*after([lat_near], *waits), lat_far, t_two, cot3, act3, hid, ghid],
            flops=flops,
            scratch=[pltpu.VMEM((chans, cells), BF16), part],
            aliases={6: 0},
        )

    ghid, keep, send = turns.run(grad_one_part)
    one = Summed(keep, send, factor)
    turns.start(one)
    turns.finish(two)
    turns.start(two)
    turns.finish(one)
    turns.start(one)
    rims = turns.run(rim_part)
    turns.finish(two)
    turns.start(two)

    results = [None, None]
    waiting = []

    def flushed(buffers):
        for (which, _, _), buffer in zip(waiting, buffers):
            results[which] = buffer
        waiting.clear()

    def flushes():
        return [(x, results[which], row, cells) for which, x, row in waiting]

    def piece(which, half, waits):
        count = rows // 2
        result, *buffers = call(
            functools.partial(last_kernel, bool(which), half * count, count),
            ("field_out", "grad_in")[which],
            [((count * cols, chans), BF16)],
            [rims[which], *after([(mid, ghid)[which]], *waits)]
            + [(k_two, t_one)[which], field, cot],
            flops=flops // 2,
            scratch=[pltpu.VMEM(((count + 2) * cols, 3 * chans), BF16)],
            flush=flushes(),
        )
        flushed(buffers)
        waiting.append((which, result, half * count * cols))
        return [result, *buffers]

    def own_half(waits):
        more = [(two.result, None, 0, 9 * chans)]
        value = after(one.sent, *waits)[0]
        result, *buffers = one.scale(value, True, flushes() + more)
        two.result = buffers.pop()
        flushed(buffers)
        return [result, *buffers, two.result]

    work = [functools.partial(piece, which, half) for which in (0, 1) for half in (0, 1)]
    for turn in (0, one, two, 1, one, two, 2, one, two, 3):
        if isinstance(turn, int):
            turns.run(work[turn])
        elif turn.steps:
            turns.finish(turn)
            if turn.steps:
                turns.start(turn)
    while len(one.steps) > 1 or two.steps:
        for chain in (one, two):
            if len(chain.steps) > 1 or chain is two and chain.steps:
                turns.finish(chain)
                if chain.steps:
                    turns.start(chain)
    turns.run(own_half)
    turns.finish(one)
    shape = (3, 3, chans, chans)
    return (
        results[0].reshape(rows, cols, chans),
        results[1].reshape(rows, cols, chans),
        one.result.reshape(shape),
        two.result.reshape(shape),
    )


def solution(mesh):
    return jax.shard_map(
        shards,
        mesh=mesh,
        in_specs=(P("lat", "lon", None), P(), P(), P("lat", "lon", None)),
        out_specs=(P("lat", "lon", None), P("lat", "lon", None), P(), P()),
        check_vma=False,
    )
```

```python
import functools

import jax
import jax.numpy as jnp
from jax import lax
from jax.experimental import pallas as pl
from jax.experimental.pallas import tpu as pltpu
from jax.sharding import PartitionSpec as P

BOTH = ("lat", "lon")
F32, BF16 = jnp.float32, jnp.bfloat16


def kernel_call(body, name, outs, ins, flops=0, scratch=(), aliases=None, limit=24, flush=()):
    outs, ins, scratch, aliases = list(outs), list(ins), list(scratch), dict(aliases or {})
    counts = len(ins), len(outs), len(scratch)
    rows, given = [], []
    for array, buffer, row, total in flush:
        ins.append(array)
        rows.append((row, array.shape[0]))
        given.append(buffer is not None)
        outs.append(((total, array.shape[1]), array.dtype, "hbm"))
        if buffer is not None:
            aliases[len(ins)] = len(outs) - 1
            ins.append(in_hbm(buffer))
        scratch.append(pltpu.SemaphoreType.DMA)
    if flush:
        body = functools.partial(flushing_kernel, body, counts, rows, given)
    out_shape, out_specs, in_specs, arrays = [], [], [], []
    for shape, kind, *spot in outs:
        out_shape.append(pltpu.HBM(shape, kind) if spot else pltpu.VMEM(shape, kind))
        out_specs.append(pl.BlockSpec(memory_space=pltpu.HBM if spot else pltpu.VMEM))
    for x in ins:
        far = isinstance(x, tuple)
        arrays.append(x[0] if far else x)
        in_specs.append(pl.BlockSpec(memory_space=pltpu.HBM if far else pltpu.VMEM))
    moved = sum(x.size * x.dtype.itemsize for x in arrays)
    return pl.pallas_call(
        body,
        out_shape=out_shape,
        in_specs=in_specs,
        out_specs=out_specs,
        scratch_shapes=scratch,
        input_output_aliases=aliases,
        compiler_params=pltpu.CompilerParams(vmem_limit_bytes=limit << 20),
        cost_estimate=pl.CostEstimate(flops=flops, bytes_accessed=moved, transcendentals=0),
        name=name,
    )(*arrays)


def flushing_kernel(body, counts, rows, given, *refs):
    refs = list(refs)

    def take(count):
        taken = refs[:count]
        del refs[:count]
        return taken

    ins = take(counts[0])
    sources = []
    for has_buffer in given:
        sources.append(take(1 + has_buffer)[0])
    outs, buffers = take(counts[1]), take(len(rows))
    scratch, sems = take(counts[2]), take(len(rows))
    copies = [
        pltpu.make_async_copy(source, buffer.at[pl.ds(row, count), :], sem)
        for source, buffer, sem, (row, count) in zip(sources, buffers, sems, rows)
    ]
    for copy in copies:
        copy.start()
    body(*ins, *outs, *scratch)
    for copy in copies:
        copy.wait()


def in_hbm(x):
    return (pltpu.with_memory_space_constraint(x, pltpu.HBM),)


def sigmoid(value):
    return 1.0 / (1.0 + jnp.exp(-value))


def silu(value):
    return value / (1.0 + jnp.exp(-value))


def same(value):
    return value


def silu_grad(value):
    sig = sigmoid(value)
    return sig * (1.0 + value * (1.0 - sig))


def aligned(start, step):
    return pl.multiple_of(start, step)


def is_odd(axis):
    return lax.axis_index(axis) % 2 == 1


def put_shifted(out, start, x, cols, left=None, right=None):
    chans = x.shape[1]
    col = lax.broadcasted_iota(jnp.int32, x.shape, 0)
    before = pltpu.roll(x, 1, 0)
    after = pltpu.roll(x, cols - 1, 0)
    if left is not None:
        before = jnp.where(col == 0, left, before)
        after = jnp.where(col == cols - 1, right, after)
    where = pl.ds(start, cols)
    out[where, :chans] = before.astype(BF16)
    out[where, chans : 2 * chans] = x.astype(BF16)
    out[where, 2 * chans :] = after.astype(BF16)


def conv_rows(shifted, weights, start, count, cols):
    piece = jnp.concatenate([shifted[pl.ds(start + i * cols, count), :] for i in range(3)], axis=1)
    return jnp.dot(piece, weights[...], preferred_element_type=F32)


def ends_kernel(cols, field_hbm, cot_hbm, field, cot, near, far, lines, sems):
    rows = field.shape[0] // cols
    copies = [
        pltpu.make_async_copy(field_hbm, field, sems.at[0]),
        pltpu.make_async_copy(cot_hbm, cot, sems.at[1]),
    ]
    for copy in copies:
        copy.start()
    odd = is_odd("lon")
    half = 4 * rows
    for n, (copy, source) in enumerate(zip(copies, (field, cot))):
        copy.wait()
        for r in range(rows):
            first = source[r * cols : r * cols + 16, :].astype(F32)
            last = source[(r + 1) * cols - 16 : (r + 1) * cols, :].astype(F32)
            for k in range(2):
                at = (2 * n + k) * rows + r
                lines[at : at + 1, :] = jnp.where(odd, first[k : k + 1], last[14 + k : 15 + k])
                at += half
                lines[at : at + 1, :] = jnp.where(odd, last[14 + k : 15 + k], first[k : k + 1])
    near[...] = lines[:half, :].astype(BF16)
    far[...] = lines[half:, :].astype(BF16)


def prep_kernel(cols, field, cot, one_hbm, two_hbm, act3, cot3, k_one, k_two, t_one, t_two, sems):
    rows = field.shape[0] // cols
    chans = field.shape[1]
    copies = [
        pltpu.make_async_copy(one_hbm, k_one, sems.at[0]),
        pltpu.make_async_copy(two_hbm, k_two, sems.at[1]),
    ]
    for copy in copies:
        copy.start()

    def body(r, carry):
        at = aligned(r * cols, cols)
        to = aligned((r + 1) * cols, cols)
        put_shifted(act3, to, silu(field[pl.ds(at, cols), :].astype(F32)), cols)
        put_shifted(cot3, to, cot[pl.ds(at, cols), :].astype(F32), cols)
        return carry

    lax.fori_loop(0, rows, body, 0, unroll=4)
    for copy in copies:
        copy.wait()
    for tap in range(9):
        to = slice((8 - tap) * chans, (9 - tap) * chans)
        at = slice(tap * chans, (tap + 1) * chans)
        t_one[to, :] = k_one[at, :].T
        t_two[to, :] = k_two[at, :].T


def edge_kernel(cols, field, cot, near, far, send_near, send_far):
    rows = field.shape[0] // cols
    chans = field.shape[1]
    odd = is_odd("lon")
    odd_lat = lax.axis_index("lat") % 2
    low, high = near[...].astype(F32), far[...].astype(F32)
    left, right = jnp.where(odd, low, high), jnp.where(odd, high, low)
    for out, first in ((send_near, odd_lat), (send_far, 1 - odd_lat)):
        start = aligned((1 - first) * (rows - 2) * cols, cols)
        out[: 2 * cols, :] = field[pl.ds(start, 2 * cols), :]
        out[2 * cols : 4 * cols, :] = cot[pl.ds(start, 2 * cols), :]
        lines = []
        for n in range(2):
            for r in range(2):
                for side in (left, right):
                    for k in range(2):
                        base = (2 * n + k) * rows
                        top = side[base + r : base + r + 1]
                        bottom = side[base + rows - 2 + r : base + rows - 1 + r]
                        lines.append(jnp.where(first == 1, top, bottom))
        out[4 * cols :, :] = jnp.concatenate(lines, axis=0).astype(BF16)


def inner_kernel(
    cols, near, far, k_one, t_two, _a, _c, act3, cot3, hid, mid, ghid, turned, edges
):
    rows = near.shape[0] // 4
    chans = near.shape[1]
    odd = is_odd("lon")
    low, high = near[...].astype(F32), far[...].astype(F32)
    edges[: 4 * rows, :] = jnp.where(odd, low, high)
    edges[4 * rows :, :] = jnp.where(odd, high, low)
    line = lax.broadcasted_iota(jnp.int32, (16, chans), 0)

    def patch(r, carry):
        start = aligned((r + 1) * cols, cols)
        end = aligned((r + 2) * cols - 16, 16)
        for out, base, fix in ((act3, 0, silu), (cot3, 2 * rows, same)):
            left = fix(edges[pl.ds(base + rows + r, 1), :]).astype(BF16).astype(F32)
            right = fix(edges[pl.ds(base + 4 * rows + r, 1), :]).astype(BF16).astype(F32)
            old = out[pl.ds(start, 16), :chans].astype(F32)
            out[pl.ds(start, 16), :chans] = jnp.where(line == 0, left, old).astype(BF16)
            old = out[pl.ds(end, 16), 2 * chans :].astype(F32)
            out[pl.ds(end, 16), 2 * chans :] = jnp.where(line == 15, right, old).astype(BF16)
        return carry

    lax.fori_loop(0, rows, patch, 0, unroll=4)
    for r, count in row_blocks(1, rows - 1):
        to = pl.ds((r + 1) * cols, count * cols)
        got = conv_rows(act3, k_one, r * cols, count * cols, cols)
        hid[to, :] = got
        mid[to, :] = silu(got).astype(BF16)
    for r, count in row_blocks(1, rows - 1):
        to = pl.ds((r + 1) * cols, count * cols)
        got = conv_rows(cot3, t_two, r * cols, count * cols, cols)
        ghid[to, :] = (got * silu_grad(hid[to, :])).astype(BF16)
    own = slice(3 * cols, (rows - 1) * cols)
    turned[:, 2 * cols : (rows - 2) * cols] = mid[own, :].T


def row_blocks(first, end):
    count = -(-(end - first) // 3)
    return [(r, min(count, end - r)) for r in range(first, end, count)]


def halo_rows(near, far):
    odd = is_odd("lat")
    low, high = near[...].astype(F32), far[...].astype(F32)
    return jnp.where(odd, low, high), jnp.where(odd, high, low)


def put_halo(part, halos, n, cols, fix, source):
    rows = source.shape[0] // cols - 2
    for half, halo in enumerate(halos):
        base = half * 4 * cols
        inside = rows - 1 if half else 1
        own = slice(inside * cols, (inside + 2) * cols)
        part[base + (1 - half) * 2 * cols : base + (2 - half) * 2 * cols, :] = source[own, :]
        for r in range(2):
            x = fix(halo[(2 * n + r) * cols : (2 * n + r + 1) * cols])
            corner = 4 * cols + 8 * n + 4 * r
            left, right = fix(halo[corner + 1 : corner + 2]), fix(halo[corner + 2 : corner + 3])
            put_shifted(part, base + (half * 2 + r) * cols, x, cols, left, right)


def edge_mask(half, cols, shape):
    lat = lax.axis_index("lat")
    there = lat < lax.axis_size("lat") - 1 if half else lat > 0
    line = lax.broadcasted_iota(jnp.int32, shape, 0)
    inner = line < cols if half else line >= cols
    return jnp.logical_or(inner, there)


def outer_kernel(
    cols, near, far, k_one, _a, _c, _h, _m, _t,
    act3, cot3, hid, mid, turned, keep, send, part,
):
    chans = mid.shape[1]
    rows = mid.shape[0] // cols - 2
    halos = halo_rows(near, far)
    put_halo(part, halos, 1, cols, same, cot3)
    cot3[:cols, :] = part[cols : 2 * cols, :]
    cot3[(rows + 1) * cols :, :] = part[6 * cols : 7 * cols, :]
    put_halo(part, halos, 0, cols, silu, act3)
    act3[:cols, :] = part[cols : 2 * cols, :]
    act3[(rows + 1) * cols :, :] = part[6 * cols : 7 * cols, :]
    for half in range(2):
        to = half * rows * cols
        got = conv_rows(part, k_one, half * 4 * cols, 2 * cols, cols)
        hid[to : to + 2 * cols, :] = got
        value = jnp.where(edge_mask(half, cols, got.shape), silu(got), 0.0)
        mid[to : to + 2 * cols, :] = value.astype(BF16)
    turned[:, : 2 * cols] = mid[cols : 3 * cols, :].T
    turned[:, (rows - 2) * cols :] = mid[(rows - 1) * cols : (rows + 1) * cols, :].T
    own = core_order(turned)
    half = chans // 2
    for i in range(3):
        got = jnp.dot(own, cot3[i * cols : (i + rows) * cols, :], preferred_element_type=F32)
        for j in range(3):
            tap = (2 - i) * 3 + 2 - j
            to, at = slice(tap * half, (tap + 1) * half), slice(j * chans, (j + 1) * chans)
            keep[to, :] = got[:half, at]
            send[to, :] = got[half:, at].astype(BF16)


def core_order(turned):
    half = turned.shape[0] // 2
    bit = lax.axis_index("lon") % 2
    mine, other = (pl.ds(aligned(x * half, 16), half) for x in (bit, 1 - bit))
    return jnp.concatenate([turned[mine, :], turned[other, :]], axis=0)


def grad_one_kernel(cols, near, far, t_two, cot3, act3, hid, _g, ghid, keep, send, turned, part):
    chans, cells = turned.shape
    rows = cells // cols
    put_halo(part, halo_rows(near, far), 1, cols, same, cot3)
    for half in range(2):
        to = slice(half * rows * cols, half * rows * cols + 2 * cols)
        got = conv_rows(part, t_two, half * 4 * cols, 2 * cols, cols)
        value = jnp.where(edge_mask(half, cols, got.shape), got * silu_grad(hid[to, :]), 0.0)
        ghid[to, :] = value.astype(BF16)
    turned[...] = ghid[cols : (rows + 1) * cols, :].T
    own = core_order(turned)
    half = chans // 2
    for i in range(3):
        got = jnp.dot(own, act3[i * cols : i * cols + cells, :], preferred_element_type=F32)
        for j in range(3):
            tap = i * 3 + j
            to, at = slice(tap * chans, (tap + 1) * chans), slice(j * chans, (j + 1) * chans)
            keep[to, :] = got[:half, at].T
            send[to, :] = got[half:, at].T.astype(BF16)


def rim_kernel(cols, own_near, own_far, near, far, lat_near, lat_far, k_one, t_two, mid, ghid):
    rows = near.shape[0] // 4
    chans = near.shape[1]
    lanes = mid.shape[0] // 2
    odd = is_odd("lon")
    pairs = [[x[...].astype(F32) for x in pair] for pair in ((own_far, own_near), (near, far))]
    (first, last), (left, right) = [
        (jnp.where(odd, b, a), jnp.where(odd, a, b)) for a, b in (pairs[0], pairs[1][::-1])
    ]
    halos = halo_rows(lat_near, lat_far)
    lat = lax.axis_index("lat")
    line = lax.broadcasted_iota(jnp.int32, (2 * lanes, chans), 0) % lanes
    inside = jnp.logical_and(
        jnp.logical_or(line > 0, lat > 0),
        jnp.logical_or(line <= rows, lat < lax.axis_size("lat") - 1),
    )

    def column(n, source, k, spot, fix):
        ends = []
        for halo in halos:
            for r in range(2):
                at = spot(n, r)
                ends.append(halo[at : at + 1])
        base = (2 * n + k) * rows
        filler = jnp.zeros((lanes - rows - 4, chans), F32)
        lines = [*ends[:2], source[base : base + rows], *ends[2:], filler]
        return fix(jnp.concatenate(lines, axis=0))

    def corner(k):
        return lambda n, r: 4 * cols + 8 * n + 4 * r + k

    def main(col):
        return lambda n, r: (2 * n + r) * cols + col

    results = []
    for n, (fix, weights) in enumerate(((silu, k_one), (same, t_two))):
        sides = []
        for spots in (
            ((left, 0, corner(0)), (left, 1, corner(1)), (first, 0, main(0))),
            ((last, 1, main(cols - 1)), (right, 0, corner(2)), (right, 1, corner(3))),
        ):
            three = jnp.concatenate(
                [column(n, source, k, spot, fix) for source, k, spot in spots], axis=1
            )
            nine = [three, pltpu.roll(three, lanes - 1, 0), pltpu.roll(three, lanes - 2, 0)]
            sides.append(jnp.concatenate(nine, axis=1))
        both = jnp.concatenate(sides, axis=0).astype(BF16)
        results.append(jnp.dot(both, weights[...], preferred_element_type=F32))
    hid, gmid = results
    mid[...] = jnp.where(inside, silu(hid), 0.0)
    ghid[...] = jnp.where(inside, gmid * silu_grad(hid), 0.0)


def last_kernel(backward, first, count, cols, edges, value, weights, field, cot, *rest):
    out, shifted = rest
    lanes = edges.shape[0] // 2

    def body(r, carry):
        x = value[pl.ds(aligned((first + r) * cols, cols), cols), :].astype(F32)
        left, right = edges[pl.ds(first + r, 1), :], edges[pl.ds(lanes + first + r, 1), :]
        put_shifted(shifted, aligned(r * cols, cols), x, cols, left, right)
        return carry

    lax.fori_loop(0, count + 2, body, 0, unroll=2)
    step = count
    for r in range(0, count, step):
        at = slice((first + r) * cols, (first + r + step) * cols)
        to = slice(r * cols, (r + step) * cols)
        got = conv_rows(shifted, weights, r * cols, step * cols, cols)
        x = field[at, :].astype(F32)
        if backward:
            out[to, :] = (cot[at, :].astype(F32) + got * silu_grad(x)).astype(BF16)
        else:
            out[to, :] = (x + got).astype(BF16)


def place():
    return lax.axis_index("lat"), lax.axis_index("lon") % 2


def partner(n):
    lat, odd = place()
    even_mask, odd_mask = group_masks(lax.axis_size("lat"))[n]
    return lat ^ jnp.where(odd == 1, odd_mask, even_mask)


def chunk(index, rows):
    return pl.ds(aligned(index * rows, 16), rows)


def spread_kernel(keep, got, own, *sends):
    rows = own.shape[0]
    at = chunk(place()[0], rows)
    own[...] = keep[at, :] + got[at, :].astype(F32)
    for n, send in enumerate(sends):
        at = chunk(partner(n), rows)
        send[...] = (keep[at, :] + got[at, :].astype(F32)).astype(BF16)


def add_round_kernel(own, *rest):
    out = rest[-1]
    total = own[...].astype(F32)
    for got in rest[:-1]:
        total = total + got[...].astype(F32)
    out[...] = total.astype(BF16)


def join_kernel(value, *rest):
    out = rest[-1]
    rows = value.shape[0]
    out[chunk(place()[0], rows), :] = value[...]
    for n, got in enumerate(rest[:-1]):
        out[chunk(partner(n), rows), :] = got[...]


def scale_kernel(factor, own, got, out):
    half = out.shape[1] // 2
    bit = lax.axis_index("lon") % 2
    for tap in range(9):
        at = slice(tap * half, (tap + 1) * half)
        for x, which in ((own, bit), (got, 1 - bit)):
            to = pl.ds(aligned((2 * tap + which) * half, 16), half)
            out[to, :] = x[at, :].astype(F32) * factor


def final_kernel(factor, own, value, *rest):
    out, scaled, sems = rest[-3:]
    rows, half = value.shape
    count = rows // sems.shape[0]
    bit = lax.axis_index("lon") % 2
    lanes = pl.ds(aligned((bit if own else 1 - bit) * half, half), half)
    copies = []
    for n in range(sems.shape[0]):
        at = pl.ds(n * count, count)
        scaled[at, :] = value[at, :].astype(F32) * factor
        copies.append(pltpu.make_async_copy(scaled.at[at, :], out.at[at, lanes], sems.at[n]))
        copies[-1].start()
    for copy in copies:
        copy.wait()


def paired(count, offset, periodic):
    pairs = []
    for low in range(offset, count, 2):
        high = low + 1
        if high == count:
            if not periodic:
                continue
            high = 0
        pairs += [(low, high), (high, low)]
    return pairs


def log2(count):
    assert count & (count - 1) == 0
    return count.bit_length() - 1


def reversed_bits(value, width):
    return int(format(value, f"0{width}b")[::-1], 2)


def group_masks(count):
    return [(k, reversed_bits(k, log2(count))) for k in range(1, count)]


def flat_pairs(lat_count, lon_count, move):
    pairs = []
    for lat in range(lat_count):
        for lon in range(lon_count):
            to_lat, to_lon = move(lat, lon)
            pairs.append((lat * lon_count + lon, to_lat * lon_count + to_lon))
    return pairs


def after(values, *others):
    return list(lax.optimization_barrier((*values, *others)))[: len(values)]


class Summed:
    def __init__(self, keep, send, factor):
        lat_count, lon_count = lax.axis_size("lat"), lax.axis_size("lon")
        self.keep, self.sent, self.factor, self.result = keep, [send], factor, None
        core = flat_pairs(lat_count, lon_count, lambda lat, lon: (lat, lon ^ 1))
        group = [
            flat_pairs(
                lat_count, lon_count, lambda lat, lon, m=m: (lat ^ (m[1] if lon & 1 else m[0]), lon)
            )
            for m in group_masks(lat_count)
        ]
        width = log2(lon_count) - 1
        line = [
            flat_pairs(
                lat_count,
                lon_count,
                lambda lat, lon, n=n: (lat, lon ^ (2 << (width - 1 - n if lon & 1 else n))),
            )
            for n in range(width)
        ]
        self.steps = [("core", [core]), ("lat", group)]
        self.steps += [("lon", [pairs]) for pairs in line]
        self.steps += [("join", group), ("last", [core])]

    def start(self):
        kind, pairs = self.steps[0]
        sent = self.sent if kind == "lat" else self.sent * len(pairs)
        self.got = [lax.ppermute(x, BOTH, p) for x, p in zip(sent, pairs)]

    def finish(self):
        kind = self.steps.pop(0)[0]
        got, (rows, chans) = self.got, self.keep.shape
        if kind == "core":
            count = lax.axis_size("lat")
            piece = rows // count
            assert piece % 16 == 0
            outs = [((piece, chans), F32)] + [((piece, chans), BF16)] * (count - 1)
            self.keep, *self.sent = kernel_call(
                spread_kernel, "spread", outs, [self.keep, *got], limit=16
            )
        elif kind == "join":
            outs = [((rows * lax.axis_size("lat"), chans), BF16)]
            self.sent = kernel_call(join_kernel, "join", outs, [*self.sent, *got], limit=16)
        elif kind == "last" and self.result is None:
            outs = [((2 * rows * lax.axis_size("lat"), chans), F32)]
            body = functools.partial(scale_kernel, self.factor)
            (self.result,) = kernel_call(body, "scaled", outs, [*self.sent, *got], limit=16)
            self.sent = [self.result]
        elif kind == "last":
            self.sent = self.scale(got[0], False)
        else:
            mine = self.keep if kind == "lat" else self.sent[0]
            outs = [((rows, chans), BF16)]
            self.sent = kernel_call(add_round_kernel, "add", outs, [mine, *got], limit=16)

    def scale(self, value, own, flush=()):
        rows, chans = value.shape
        ins = [value] if own else [value, in_hbm(self.result)]
        self.result, *buffers = kernel_call(
            functools.partial(final_kernel, self.factor, own),
            "scaled",
            [((rows, 2 * chans), F32, "hbm")],
            ins,
            scratch=[pltpu.VMEM((rows, chans), F32), pltpu.SemaphoreType.DMA((4,))],
            aliases=None if own else {1: 0},
            limit=16,
            flush=flush,
        )
        return [self.result, *buffers]


class Turns:
    def __init__(self):
        self.last = []

    def run(self, work):
        result = work(self.last)
        self.last = list(result)
        return result

    def start(self, chain):
        chain.sent = after(chain.sent, *self.last)
        self.last = list(chain.sent)
        chain.start()

    def finish(self, chain):
        chain.got = after(chain.got, *self.last)
        chain.finish()
        self.last = list(chain.sent)


def shards(field_in, kernel_one, kernel_two, cotangent):
    rows, cols, chans = field_in.shape
    cells, tall = rows * cols, (rows + 2) * cols
    lat_count, lon_count = lax.axis_size("lat"), lax.axis_size("lon")
    factor = float(rows * lat_count * cols * lon_count) ** (-0.5)
    flops = 2 * cells * 9 * chans * chans
    sems = pltpu.SemaphoreType.DMA((2,))

    def call(body, *args, **kwargs):
        return kernel_call(functools.partial(body, cols), *args, **kwargs)

    near_lon, far_lon = paired(lon_count, 0, True), paired(lon_count, 1, True)
    near_lat, far_lat = paired(lat_count, 0, False), paired(lat_count, 1, False)

    tile = ((cells, chans), BF16)
    line = ((4 * rows, chans), BF16)
    field, cot, near, far = call(
        ends_kernel,
        "ends",
        [tile, tile, line, line],
        [in_hbm(field_in.reshape(cells, chans)), in_hbm(cotangent.reshape(cells, chans))],
        scratch=[pltpu.VMEM((8 * rows, chans), F32), sems],
    )
    lon_far = lax.ppermute(far, "lon", far_lon)
    wide = ((tall, 3 * chans), BF16)
    square = ((9 * chans, chans), BF16)
    act3, cot3, k_one, k_two, t_one, t_two = call(
        prep_kernel,
        "prep",
        [wide, wide, square, square, square, square],
        [field, cot] + [in_hbm(k.reshape(9 * chans, chans)) for k in (kernel_one, kernel_two)],
        flops=flops,
        scratch=[sems],
    )

    lon_near = lax.ppermute(after([near], act3)[0], "lon", near_lon)

    strip = ((4 * cols + 16, chans), BF16)
    send_near, send_far = call(
        edge_kernel, "edges", [strip, strip], [field, cot, *after([lon_near, lon_far], act3)]
    )
    lat_near = lax.ppermute(send_near, "lat", near_lat)
    lat_far = lax.ppermute(send_far, "lat", far_lat)

    high = ((tall, chans), F32)
    flat = ((tall, chans), BF16)
    turned = ((chans, cells), BF16)
    act3, cot3, hid, mid, ghid, mid_t = call(
        inner_kernel,
        "inner_rows",
        [wide, wide, high, flat, flat, turned],
        [lon_near, lon_far, k_one, t_two, *after([act3], send_near, send_far), cot3],
        flops=2 * flops,
        scratch=[pltpu.VMEM((8 * rows, chans), F32)],
        aliases={4: 0, 5: 1},
    )
    half = (9 * chans // 2, chans)
    parts = [(half, F32), (half, BF16)]
    part = pltpu.VMEM((8 * cols, 3 * chans), BF16)
    act3, cot3, hid, mid, _, keep, send = call(
        outer_kernel,
        "grad_two",
        [wide, wide, high, flat, turned] + parts,
        [lat_near, lat_far, k_one, act3, cot3, hid, mid, mid_t],
        flops=flops,
        scratch=[part],
        aliases={3: 0, 4: 1, 5: 2, 6: 3, 7: 4},
    )
    turns = Turns()
    two = Summed(keep, send, factor)
    turns.start(two)

    lanes = -(-(rows + 4) // 8) * 8
    rim = ((2 * lanes, chans), F32)

    def rim_part(waits):
        return call(
            rim_kernel,
            "rim",
            [rim, rim],
            [near, far, *after([lon_near, lon_far], *waits), lat_near, lat_far, k_one, t_two],
            flops=flops // 16,
        )

    def grad_one_part(waits):
        return call(
            grad_one_kernel,
            "grad_one",
            [flat] + [((9 * chans, chans // 2), kind) for kind in (F32, BF16)],
            [*after([lat_near], *waits), lat_far, t_two, cot3, act3, hid, ghid],
            flops=flops,
            scratch=[pltpu.VMEM((chans, cells), BF16), part],
            aliases={6: 0},
        )

    ghid, keep, send = turns.run(grad_one_part)
    one = Summed(keep, send, factor)
    turns.start(one)
    turns.finish(two)
    turns.start(two)
    turns.finish(one)
    turns.start(one)
    rims = turns.run(rim_part)
    turns.finish(two)
    turns.start(two)

    results = [None, None]
    waiting = []

    def flushed(buffers):
        for (which, _, _), buffer in zip(waiting, buffers):
            results[which] = buffer
        waiting.clear()

    def flushes():
        return [(x, results[which], row, cells) for which, x, row in waiting]

    def piece(which, half, waits):
        count = rows // 2
        result, *buffers = call(
            functools.partial(last_kernel, bool(which), half * count, count),
            ("field_out", "grad_in")[which],
            [((count * cols, chans), BF16)],
            [rims[which], *after([(mid, ghid)[which]], *waits)]
            + [(k_two, t_one)[which], field, cot],
            flops=flops // 2,
            scratch=[pltpu.VMEM(((count + 2) * cols, 3 * chans), BF16)],
            flush=flushes(),
        )
        flushed(buffers)
        waiting.append((which, result, half * count * cols))
        return [result, *buffers]

    def own_half(waits):
        more = [(two.result, None, 0, 9 * chans)]
        value = after(one.sent, *waits)[0]
        result, *buffers = one.scale(value, True, flushes() + more)
        two.result = buffers.pop()
        flushed(buffers)
        return [result, *buffers, two.result]

    work = [functools.partial(piece, which, half) for which in (0, 1) for half in (0, 1)]
    for turn in (0, one, two, 1, one, two, 2, one, two, 3):
        if isinstance(turn, int):
            turns.run(work[turn])
        elif turn.steps:
            turns.finish(turn)
            if turn.steps:
                turns.start(turn)
    while len(one.steps) > 1 or two.steps:
        for chain in (one, two):
            if len(chain.steps) > 1 or chain is two and chain.steps:
                turns.finish(chain)
                if chain.steps:
                    turns.start(chain)
    turns.run(own_half)
    turns.finish(one)
    shape = (3, 3, chans, chans)
    return (
        results[0].reshape(rows, cols, chans),
        results[1].reshape(rows, cols, chans),
        one.result.reshape(shape),
        two.result.reshape(shape),
    )


def solution(mesh):
    return jax.shard_map(
        shards,
        mesh=mesh,
        in_specs=(P("lat", "lon", None), P(), P(), P("lat", "lon", None)),
        out_specs=(P("lat", "lon", None), P("lat", "lon", None), P(), P()),
        check_vma=False,
    )
```
